256 devices in a mesh: grp: 8 (over x, core), dev: 32 (over y, z).
Axes of the slice: x: 4, y: 4, z: 8, core: 2. Of those that a mesh axis runs over, the one named last changes fastest.
Arguments:
- enc_tokens: bfloat16 [8, 64, 192, 1024], P('grp', 'dev'), may hold values from -8 to 8
- focal_len: bfloat16 [8, 64], P('grp', 'dev'), may hold values from 6 to 20
- depth_map: bfloat16 [8, 64, 192], P('grp', 'dev'), may hold values from 0.5 to 4
- cameras: bfloat16 [8, 64, 12], P('grp', 'dev'), may hold values from -3 to 3
- pair_graph: int32 [8, 128, 2], P('grp'), may hold values from 0 to 63, as said below
- pair_params: float32 [8, 128, 13], P('grp', 'dev'), may hold values from -3 to 3
- embed_weight: bfloat16 [1024, 768], replicated, may hold values from -0.1875 to 0.1875
- cross_query: bfloat16 [2, 768, 768], replicated, may hold values from -4 to 4
- cross_keyval: bfloat16 [2, 768, 1536], replicated, may hold values from -4 to 4
- cross_out: bfloat16 [2, 768, 768], replicated, may hold values from -0.21875 to 0.21875
- point_heads: bfloat16 [2, 768, 4], replicated, may hold values from -0.21875 to 0.21875
Outputs:
- pair_points: float32 [8, 128, 2, 4, 192], P('grp', 'dev')
- new_depth: float32 [8, 64, 192], P('grp', 'dev')
- new_cameras: float32 [8, 64, 12], P('grp', 'dev')
- new_pair_params: float32 [8, 128, 13], P('grp', 'dev')
The draws below stay inside these ranges and needn't reach their ends.
Inputs may be any that keep to these rules, and one draw needn't show every extreme that they name: `pair_graph`: pair e of a group is served by device e // 4 of that group's dev axis; image i lies with device i // 2. The 8 images named by one device's 4 pairs lie with 8 different devices.
All inputs are finite; a program needn't handle non-finite values.
Results may differ from the reference program's by a relative error of at most 0.014.
Values may be sent and summed in bfloat16 or wider, within the bound.
No kernel may reach another device: no remote copies, remote signals or barrier semaphores. Data moves between devices by JAX's collectives and lax.ppermute only.
A program may use at most 128 MiB of HBM per device.

```python
import math
import jax
import jax.numpy as jnp
from jax import lax

E = 1024
HEADS = 12
HD = 64
DD = 768
TOK = 192
GW = 16
IMG_DEV = 2
PAIR_DEV = 4
IMG_GRP = 64
PAIRS = 128
N_GRP = 8
N_DEV = 32


def shared_query(key):
    return jax.random.normal(key, (2, DD, DD), jnp.float32)


def draw_enc_tokens(key, part):
    key = jax.random.fold_in(key, 3)
    noise_key = jax.random.fold_in(key, 0)
    noise = jax.random.normal(noise_key, (N_GRP, IMG_GRP, TOK, E), jnp.float32)
    return jnp.clip(noise, -8.0, 8.0).astype(jnp.bfloat16)


def draw_cross_query(key, part):
    shared = shared_query(key)
    return jnp.clip(shared * (1.0 / math.sqrt(DD)), -4.0, 4.0).astype(jnp.bfloat16)


def draw_cross_keyval(key, part):
    key = jax.random.fold_in(key, 7)
    key_part, value_part = jax.random.split(key, 2)
    value_rows = jax.random.normal(value_part, (2, DD, DD), jnp.float32) * (1.0 / math.sqrt(DD))
    key_rows = jax.random.normal(key_part, (2, DD, DD), jnp.float32) * (1.0 / math.sqrt(DD))
    return jnp.clip(jnp.concatenate([key_rows, value_rows], axis=-1), -4.0, 4.0).astype(jnp.bfloat16)


def draw_pair_graph(key, part):
    key = jax.random.fold_in(key, 11)
    hot_key, noise_key, local_key = jax.random.split(key, 3)
    hotness = jax.random.randint(hot_key, (N_GRP, 1, N_DEV), 0, 4, jnp.int32)
    jitter = jax.random.randint(noise_key, (N_GRP, N_DEV, N_DEV), 0, 1024, jnp.int32)
    owner_ids = jnp.arange(N_DEV, dtype=jnp.int32)
    ranking = (hotness * 1024 + jitter) * N_DEV + owner_ids
    unused, chosen = lax.top_k(ranking, 2 * PAIR_DEV)
    local_pick = jax.random.randint(local_key, chosen.shape, 0, IMG_DEV, jnp.int32)
    images = chosen.astype(jnp.int32) * IMG_DEV + local_pick
    return images.reshape(N_GRP, PAIR_DEV * N_DEV, 2).astype(jnp.int32)


def levels(rng, extent, pieces, least, largest):
    factor_of = 1.0
    for dim, blocks in pieces:
        draws = jax.random.uniform(jax.random.fold_in(jax.random.fold_in(rng, 6), dim), (blocks,), jnp.float32, least / len(pieces), largest / len(pieces))
        factor_of = factor_of * jnp.repeat(jnp.exp(draws), extent[dim] // blocks).reshape((-1,) + (1,) * (len(extent) - 1 - dim))
    return factor_of


def scatter_about(rng, dims, scale, reach, shards=(), kind=jnp.bfloat16):
    result = jax.random.normal(rng, dims, jnp.float32) * scale
    if len(shards) > 0:
        result = levels(rng, dims, shards, -0.22, 0.18) * result
    return jnp.clip(result, min=-reach, max=reach).astype(kind)


def setup_inputs(seed: int = 0) -> dict:
    keys = jax.random.split(jax.random.key(seed), 12)
    return {
        "enc_tokens": draw_enc_tokens(jax.random.fold_in(keys[11], 71), 0),
        "focal_len": jnp.clip(jnp.exp(math.log(20.0) - 1.2039728 * jax.random.uniform(keys[1], (N_GRP, IMG_GRP), jnp.float32) ** levels(keys[1], (N_GRP, IMG_GRP), ((0, 8), (1, 32)), -0.2, 0.2)), 6.0, 20.0).astype(jnp.bfloat16),
        "depth_map": jnp.clip(jnp.exp(math.log(4.0) - 2.0794415 * jax.random.uniform(keys[2], (N_GRP, IMG_GRP, TOK), jnp.float32) ** levels(keys[2], (N_GRP, IMG_GRP, TOK), ((0, 8), (1, 32)), -0.2, 0.2)), 0.5, 4.0).astype(jnp.bfloat16),
        "cameras": scatter_about(keys[3], (N_GRP, IMG_GRP, 12), 0.6, 3.0, ((0, 8), (1, 32))),
        "pair_graph": draw_pair_graph(jax.random.fold_in(keys[11], 71), 0),
        "pair_params": scatter_about(keys[5], (N_GRP, PAIRS, 13), 0.6, 3.0, ((0, 8), (1, 32)), jnp.float32),
        "embed_weight": scatter_about(keys[6], (E, DD), E ** -0.5, 0.1875),
        "cross_query": draw_cross_query(jax.random.fold_in(keys[11], 71), 0),
        "cross_keyval": draw_cross_keyval(jax.random.fold_in(keys[11], 71), 0),
        "cross_out": scatter_about(keys[9], (2, DD, DD), DD ** -0.5, 0.21875),
        "point_heads": scatter_about(keys[10], (2, DD, 4), DD ** -0.5, 0.21875),
    }


norm_eps = 1e-06
stat_eps = 1e-06
step_rate = 0.3

def layer_norm(values_in):
    centre = lax.optimization_barrier(jnp.mean(values_in, axis=-1, keepdims=True))
    centred = values_in - centre
    spread = lax.optimization_barrier(jnp.mean(centred * centred, axis=-1, keepdims=True))
    return centred * lax.rsqrt(spread + norm_eps)

def ray_table(focal_in, tok_count, grid_width):
    patch = jnp.arange(tok_count, dtype=jnp.int32)
    column = (patch % grid_width).astype(jnp.float32) - (grid_width - 1) / 2.0
    row_pos = (patch // grid_width).astype(jnp.float32) - (tok_count // grid_width - 1) / 2.0
    focal_col = focal_in[..., None]
    across = column / focal_col
    down = row_pos / focal_col
    return jnp.stack([across, down, jnp.ones_like(across)], axis=-2)

def view_terms(depth_row, camera, focal_in, points, confidence, params):
    tok_count = depth_row.shape[-1]
    ray = ray_table(focal_in, tok_count, GW)
    cam_mat = camera[..., :9].reshape(camera.shape[:-1] + (3, 3))
    cam_shift = camera[..., 9:12]
    cam_points = depth_row[..., None, :] * ray
    world = lax.optimization_barrier(jnp.sum(cam_mat[..., :, :, None] * cam_points[..., None, :, :], axis=-2)) + cam_shift[..., None]
    pair_scale = params[..., 0]
    pair_mat = params[..., 1:10].reshape(params.shape[:-1] + (3, 3))
    pair_shift = params[..., 10:13]
    fitted = lax.optimization_barrier(jnp.sum(pair_mat[..., :, :, None] * points[..., None, :, :], axis=-2)) + pair_shift[..., None]
    residual = world - pair_scale[..., None, None] * fitted
    weighted = (2.0 * confidence)[..., None, :] * residual
    ray_image = lax.optimization_barrier(jnp.sum(cam_mat[..., :, :, None] * ray[..., None, :, :], axis=-2))
    grad_depth = lax.optimization_barrier(jnp.sum(weighted * ray_image, axis=-2))
    grad_mat = lax.optimization_barrier(jnp.sum(weighted[..., :, None, :] * cam_points[..., None, :, :], axis=-1))
    grad_shift = lax.optimization_barrier(jnp.sum(weighted, axis=-1))
    grad_scale = -lax.optimization_barrier(jnp.sum(weighted * fitted, axis=(-2, -1)))
    grad_pmat = -pair_scale[..., None, None] * lax.optimization_barrier(jnp.sum(weighted[..., :, None, :] * points[..., None, :, :], axis=-1))
    grad_pshift = -pair_scale[..., None] * lax.optimization_barrier(jnp.sum(weighted, axis=-1))
    grad_cam = jnp.concatenate([grad_mat.reshape(grad_mat.shape[:-2] + (9,)), grad_shift], axis=-1)
    grad_pair = jnp.concatenate([grad_scale[..., None], grad_pmat.reshape(grad_pmat.shape[:-2] + (9,)), grad_pshift], axis=-1)
    return (grad_depth, grad_cam, grad_pair)

def attend_pair(query, memory, w_query, w_keyval, w_out, w_head):
    tok_count, dec_width = query.shape
    normed_query = layer_norm(query.astype(jnp.float32)).astype(jnp.bfloat16)
    normed_memory = layer_norm(memory.astype(jnp.float32)).astype(jnp.bfloat16)
    query_proj = jnp.dot(normed_query, w_query, preferred_element_type=jnp.float32).astype(jnp.bfloat16)
    keyval = jnp.dot(normed_memory, w_keyval, preferred_element_type=jnp.float32).astype(jnp.bfloat16)
    query_heads = query_proj.reshape(tok_count, HEADS, HD).astype(jnp.float32)
    key_heads = keyval[:, :dec_width].reshape(tok_count, HEADS, HD).astype(jnp.float32)
    value_heads = keyval[:, dec_width:].reshape(tok_count, HEADS, HD).astype(jnp.float32)
    scores = jnp.einsum('qhd,khd->hqk', query_heads, key_heads) * (1.0 / math.sqrt(HD))
    attn_probs = jax.nn.softmax(scores, axis=-1).astype(jnp.bfloat16)
    context = jnp.einsum('hqk,khd->qhd', attn_probs.astype(jnp.float32), value_heads)
    context = context.astype(jnp.bfloat16).reshape(tok_count, dec_width)
    updated = query.astype(jnp.float32) + jnp.dot(context, w_out, preferred_element_type=jnp.float32)
    decoded = updated.astype(jnp.bfloat16)
    return jnp.dot(decoded, w_head, preferred_element_type=jnp.float32)

def reference(enc_tokens, focal_len, depth_map, cameras, pair_graph, pair_params, embed_weight, cross_query, cross_keyval, cross_out, point_heads):

    def first_view(both):
        return attend_pair(both[0], both[1], cross_query[0], cross_keyval[0], cross_out[0], point_heads[0])

    def second_view(both):
        return attend_pair(both[0], both[1], cross_query[1], cross_keyval[1], cross_out[1], point_heads[1])

    def group_terms(group_in):
        tokens_in, focal_in, depth_in, camera_in, graph_in, params_in = group_in
        emb = jnp.dot(tokens_in, embed_weight, preferred_element_type=jnp.float32).astype(jnp.bfloat16)
        query_emb = emb[graph_in[:, 0]]
        memory_emb = emb[graph_in[:, 1]]
        outs_first = lax.map(first_view, (query_emb, memory_emb))
        outs_second = lax.map(second_view, (memory_emb, query_emb))
        head_rows = jnp.swapaxes(jnp.stack([outs_first, outs_second], axis=1), 2, 3)
        points = head_rows[:, :, :3]
        confidence = 1.0 + jnp.exp(head_rows[:, :, 3])
        points_out = jnp.concatenate([points, confidence[:, :, None]], axis=2)
        grad_depth, grad_cam, grad_pair = view_terms(depth_in.astype(jnp.float32)[graph_in], camera_in.astype(jnp.float32)[graph_in], focal_in.astype(jnp.float32)[graph_in], points, confidence, params_in[:, None, :])
        flat_ids = graph_in.reshape(-1)
        image_depth = jax.ops.segment_sum(grad_depth.reshape(-1, TOK), flat_ids, num_segments=IMG_GRP)
        image_cam = jax.ops.segment_sum(grad_cam.reshape(-1, 12), flat_ids, num_segments=IMG_GRP)
        return (points_out, image_depth, image_cam, lax.optimization_barrier(jnp.sum(grad_pair, axis=1)))
    pair_points, image_depth, image_cam, pair_grad = lax.map(group_terms, (enc_tokens, focal_len, depth_map, cameras, pair_graph, pair_params))
    grad_total = jnp.sum(image_depth * image_depth) + jnp.sum(image_cam * image_cam) + jnp.sum(pair_grad * pair_grad)
    param_count = N_GRP * (IMG_GRP * (TOK + 12) + 13 * PAIRS)
    step_size = step_rate / jnp.sqrt(grad_total / param_count + stat_eps)
    new_depth = depth_map.astype(jnp.float32) - step_size * image_depth
    new_cameras = cameras.astype(jnp.float32) - step_size * image_cam
    new_pair_params = pair_params - step_size * pair_grad
    return (pair_points, new_depth, new_cameras, new_pair_params)
```

```python
import functools
import math

import jax
import jax.numpy as jnp
import numpy as np
from jax import lax
from jax.experimental import pallas as pl
from jax.experimental.pallas import tpu as pltpu
from jax.sharding import PartitionSpec as P

HEADS = 12
HD = 64
DD = 768
TOK = 192
GW = 16
PEERS = 32
ROWS = TOK // PEERS
SPREAD = 16
REFS = 8
PAIRS = 4

norm_eps = 1e-06
stat_eps = 1e-06
step_rate = 0.3

F32 = jnp.float32
BF16 = jnp.bfloat16
NT = (((1,), (1,)), ((), ()))
MIB = 1024 * 1024


def params_for(mib):
    return pltpu.CompilerParams(vmem_limit_bytes=mib * MIB)


def dot(left, right):
    return jnp.dot(left, right, preferred_element_type=F32)


def dot_nt(left, right):
    return lax.dot_general(left, right, NT, preferred_element_type=F32)


def spread_order():
    table = np.zeros((8 * SPREAD, 112), np.float32)
    for peer in range(8):
        for row in range(ROWS):
            table[peer * SPREAD + row, peer * ROWS + row] = 1
            table[peer * SPREAD + ROWS + row, 48 + peer * ROWS + row] = 1
        table[peer * SPREAD + 2 * ROWS, 96] = 1
        table[peer * SPREAD + 2 * ROWS + 1, 97] = 1
    return jnp.asarray(table, BF16)


def gather_order():
    table = np.zeros((384, 384), np.float32)
    for image in range(REFS):
        for source in range(8):
            for row in range(ROWS):
                table[image * 48 + source * ROWS + row, source * 48 + image * ROWS + row] = 1
    return jnp.asarray(table, BF16)


def embed_kernel(tokens_ref, weight_ref, geo_ref, order_ref, out_ref, emb_ref):
    emb_ref[...] = dot(tokens_ref[...], weight_ref[...]).astype(BF16)
    for part in range(4):
        rows = jnp.concatenate(
            [emb_ref[part * 48 : part * 48 + 48], emb_ref[TOK + part * 48 : TOK + part * 48 + 48], geo_ref[...]],
            axis=0,
        )
        out_ref[part * 128 : (part + 1) * 128] = dot(order_ref[...], rows).astype(BF16)


def select_kernel(rows_ref, where_ref, own_ref, out_ref, geo_ref):
    total = rows_ref.shape[0]
    lane = lax.broadcasted_iota(jnp.int32, (TOK, total), 1)

    @pl.loop(0, PEERS * REFS * ROWS // TOK)
    def _(step):
        at = pl.ds(pl.multiple_of(step * TOK, TOK), TOK)
        pick = jnp.where(where_ref[at, :][:, :1] == lane, 1.0, 0.0).astype(BF16)
        out_ref[at, :] = dot(pick, rows_ref[...]).astype(BF16)

    own_lane = lax.broadcasted_iota(jnp.int32, (16, total), 1)
    own = jnp.where(own_ref[...][:, :1] == own_lane, 1.0, 0.0).astype(BF16)
    geo_ref[...] = dot(own, rows_ref[:, 0:256])[0:REFS]


def fold_kernel(head_ref, out_ref, value_ref, fold_ref):
    sub = lax.broadcasted_iota(jnp.int32, (16, DD), 0)
    lane = lax.broadcasted_iota(jnp.int32, (16, DD), 1)
    for view in range(2):
        both = dot_nt(head_ref[view], out_ref[view])
        high = both.astype(BF16).astype(F32)
        low = (both - high).astype(BF16).astype(F32)
        pair = jnp.concatenate([high[0:8], low[0:8]], axis=0)
        left = jnp.concatenate(
            [jnp.where(lane // HD == head, pair, 0.0).astype(BF16) for head in range(HEADS)], axis=0
        )
        full = dot_nt(left, value_ref[view])
        for head in range(HEADS):
            term = full[head * 16 : head * 16 + 8] + full[head * 16 + 8 : head * 16 + 16]
            top = term.astype(BF16).astype(F32)
            rest = term - top
            fold_ref[view, head * 16 : head * 16 + 16] = jnp.concatenate([top, rest], axis=0).astype(BF16)


def view_gradients(outs, geo, par):
    token = lax.broadcasted_iota(jnp.int32, (REFS, TOK), 1)
    column = (token & (GW - 1)).astype(F32) - (GW - 1) / 2.0
    row_pos = (token >> 4).astype(F32) - (TOK // GW - 1) / 2.0
    depth = geo[:, 0:TOK]
    cam = [geo[:, TOK + i : TOK + i + 1] for i in range(12)]
    focal = geo[:, TOK + 12 : TOK + 13]
    ray = [column / focal, row_pos / focal, jnp.ones_like(column)]
    cam_points = [depth * ray[0], depth * ray[1], depth]
    scale = par[:, 0:1]
    mat = [par[:, 1 + i : 2 + i] for i in range(9)]
    shift = [par[:, 10 + i : 11 + i] for i in range(3)]
    points = outs[:3]
    confidence = outs[3]
    fitted, weighted, ray_image = [], [], []
    for r in range(3):
        world = cam[3 * r] * cam_points[0] + cam[3 * r + 1] * cam_points[1] + cam[3 * r + 2] * cam_points[2]
        world = world + cam[9 + r]
        fit = mat[3 * r] * points[0] + mat[3 * r + 1] * points[1] + mat[3 * r + 2] * points[2] + shift[r]
        fitted.append(fit)
        weighted.append((2.0 * confidence) * (world - scale * fit))
        ray_image.append(cam[3 * r] * ray[0] + cam[3 * r + 1] * ray[1] + cam[3 * r + 2])
    grad_depth = weighted[0] * ray_image[0] + weighted[1] * ray_image[1] + weighted[2] * ray_image[2]

    def total(x):
        return jnp.sum(x, axis=1, keepdims=True)

    sums = [total(w) for w in weighted]
    entries = [total(weighted[r] * cam_points[c]) for r in range(3) for c in range(3)] + sums
    entries.append(-total(weighted[0] * fitted[0] + weighted[1] * fitted[1] + weighted[2] * fitted[2]))
    entries += [-scale * total(weighted[r] * points[c]) for r in range(3) for c in range(3)]
    entries += [-scale * s for s in sums]
    lane = lax.broadcasted_iota(jnp.int32, (REFS, 64), 1)
    tail = jnp.zeros((REFS, 64), F32)
    for i, entry in enumerate(entries):
        tail = jnp.where(lane == i, entry, tail)
    return grad_depth, tail


def decode_kernel(
    rows_ref, order_ref, query_ref, key_ref, fold_ref, head_ref, geo_ref, par_ref,
    points_ref, grad_ref, x_ref, n_ref, q_ref, k_ref, u_ref, e_ref, o_ref,
):
    for part in range(4):
        mixed = dot(order_ref[...], rows_ref[part * 384 : (part + 1) * 384]).astype(BF16)
        for image in range(REFS):
            at = (image // 2) * TOK + part * 48
            x_ref[image % 2, at : at + 48] = mixed[image * 48 : image * 48 + 48]

    for slot in range(2):
        @pl.loop(0, PAIRS)
        def _(pair):
            at = pl.ds(pl.multiple_of(pair * TOK, TOK), TOK)
            wide = x_ref[slot, at, :].astype(F32)
            centred = wide - jnp.mean(wide, axis=-1, keepdims=True)
            spread = jnp.mean(centred * centred, axis=-1, keepdims=True)
            n_ref[slot, at, :] = (centred * lax.rsqrt(spread + norm_eps)).astype(BF16)

    ones_row = jnp.where(lax.broadcasted_iota(jnp.int32, (8, TOK), 0) == 4, 1.0, 0.0)
    for view in range(2):
        @pl.loop(0, PAIRS)
        def _(pair):
            at = pl.ds(pl.multiple_of(pair * TOK, TOK), TOK)
            query = n_ref[view, at, :]
            memory = n_ref[1 - view, at, :]
            q_ref[view, at, :] = dot(query, query_ref[view]).astype(BF16)
            k_ref[view, at, :] = dot(memory, key_ref[view]).astype(BF16)
            value = dot_nt(fold_ref[view], memory)
            for head in range(HEADS):
                term = value[head * 16 : head * 16 + 8] + value[head * 16 + 8 : head * 16 + 16] + ones_row
                u_ref[view, pair, head * 16 : head * 16 + 16] = jnp.concatenate(
                    [term, jnp.zeros_like(term)], axis=0
                ).astype(BF16)
            e_ref[view, pair] = dot_nt(head_ref[view], x_ref[view, at, :])[0:8]

    upper = lax.broadcasted_iota(jnp.int32, (TOK, 2 * HD), 1) >= HD
    factor = math.log2(math.e) / math.sqrt(HD)
    for view in range(2):
        @pl.loop(0, PAIRS)
        def _(pair):
            at = pl.ds(pl.multiple_of(pair * TOK, TOK), TOK)
            acc = e_ref[view, pair]
            for two in range(HEADS // 2):
                cols = slice(two * 2 * HD, (two + 1) * 2 * HD)
                keys = k_ref[view, at, cols]
                queries = q_ref[view, at, cols]
                for half in range(2):
                    head = 2 * two + half
                    part = jnp.where(upper if half else jnp.logical_not(upper), queries, jnp.zeros_like(queries))
                    scores = dot_nt(keys, part)
                    top = jnp.max(scores, axis=0, keepdims=True)
                    probs = jnp.exp2((scores - top) * factor).astype(BF16)
                    mixed = dot(u_ref[view, pair, head * 16 : head * 16 + 16], probs)[0:8]
                    acc = acc + mixed * (1.0 / mixed[4:5])
            sub = lax.broadcasted_iota(jnp.int32, (8, TOK), 0)
            acc = jnp.where(sub == 3, 1.0 + jnp.exp(acc), acc)
            points_ref[2 * pair + view] = acc[0:4]
            for c in range(4):
                o_ref[c, pl.ds(2 * pair + view, 1), :] = acc[c : c + 1]

    grad_depth, tail = view_gradients([o_ref[c] for c in range(4)], geo_ref[...], par_ref[...])
    both = jnp.concatenate([grad_depth, tail], axis=1)
    for peer in range(PEERS):
        grad_ref[peer * REFS : (peer + 1) * REFS] = both


def split_dot(pick, wide):
    high = wide.astype(BF16)
    rest = wide - high.astype(F32)
    middle = rest.astype(BF16)
    low = (rest - middle.astype(F32)).astype(BF16)
    return dot(pick, high) + dot(pick, middle) + dot(pick, low)


def combine_kernel(me_ref, graph_ref, grad_ref, own_ref, square_ref):
    refs = PEERS * REFS
    me = me_ref[0]
    graph = graph_ref[...]
    grads = grad_ref[...]
    image = lax.broadcasted_iota(jnp.int32, (2 * PEERS, refs), 0)
    image_sum = split_dot(jnp.where(graph == image, 1.0, 0.0).astype(BF16), grads)
    pair = lax.broadcasted_iota(jnp.int32, (refs // 2, refs), 0)
    view = lax.broadcasted_iota(jnp.int32, (refs // 2, refs), 1)
    pair_sum = split_dot(jnp.where((view >> 1) == pair, 1.0, 0.0).astype(BF16), grads)
    image_lane = lax.broadcasted_iota(jnp.int32, (2 * PEERS, 256), 1)
    pair_lane = lax.broadcasted_iota(jnp.int32, (refs // 2, 256), 1)
    image_sq = jnp.where(image_lane < TOK + 12, image_sum * image_sum, 0.0)
    pair_sq = jnp.where((pair_lane >= TOK + 12) & (pair_lane < TOK + 25), pair_sum * pair_sum, 0.0)
    square = jnp.sum(image_sq) + jnp.sum(pair_sq)
    square_ref[...] = jnp.full((1, 128), square, F32)
    row = lax.broadcasted_iota(jnp.int32, (16, refs), 0)
    ref = lax.broadcasted_iota(jnp.int32, (16, refs), 1)
    own_image = (row < 2) & (graph == 2 * me + row)
    own_pair = (row >= 8) & (row < 8 + PAIRS) & ((ref >> 1) == PAIRS * me + row - 8)
    own_ref[...] = split_dot(jnp.where(own_image | own_pair, 1.0, 0.0).astype(BF16), grads)


def update_kernel(count, square_ref, own_ref, depth_ref, camera_ref, par_ref, depth_out, camera_out, par_out):
    total = jnp.sum(square_ref[...], axis=0, keepdims=True)[:, 0:1]
    step = step_rate / jnp.sqrt(total / count + stat_eps)
    depth_out[...] = depth_ref[...].astype(F32) - step * own_ref[0:2, 0:TOK]
    camera_out[...] = camera_ref[...].astype(F32) - step * own_ref[0:2, TOK : TOK + 12]
    par_out[...] = par_ref[...] - step * own_ref[8 : 8 + PAIRS, TOK + 12 : TOK + 25]


def shape(dims, kind):
    return jax.ShapeDtypeStruct(dims, kind)


def whole():
    return pl.BlockSpec(memory_space=pltpu.VMEM)


def on_device(
    enc_tokens, focal_len, depth_map, cameras, pair_graph, pair_params,
    embed_weight, cross_query, cross_keyval, cross_out, point_heads,
):
    me = lax.axis_index("dev")
    tokens = enc_tokens[0].reshape(2 * TOK, -1)
    geo = jnp.concatenate([depth_map[0], cameras[0], focal_len[0][:, None]], axis=1)
    geo = jnp.pad(geo, ((0, 14), (0, DD - geo.shape[1])))
    message = pl.pallas_call(
        embed_kernel,
        out_shape=shape((PEERS * SPREAD, DD), BF16),
        scratch_shapes=[pltpu.VMEM((2 * TOK, DD), BF16)],
        compiler_params=params_for(24),
        name="embed",
    )(tokens, embed_weight, geo, spread_order())
    spread = lax.all_to_all(message, "dev", split_axis=0, concat_axis=0, tiled=True)

    graph = pair_graph[0].reshape(PEERS * REFS)
    first = (graph // 2) * SPREAD + (graph % 2) * ROWS
    where = (first[:, None] + jnp.arange(ROWS, dtype=jnp.int32)[None, :]).reshape(-1, 1)
    mine = lax.dynamic_slice_in_dim(graph, me * REFS, REFS)
    own = jnp.pad((mine // 2) * SPREAD + 2 * ROWS + mine % 2, (0, 8))[:, None]
    head_rows = jnp.pad(jnp.swapaxes(point_heads, 1, 2), ((0, 0), (0, 12), (0, 0)))
    outgoing, my_geo = pl.pallas_call(
        select_kernel,
        out_shape=(shape((PEERS * REFS * ROWS, DD), BF16), shape((REFS, 256), F32)),
        compiler_params=params_for(24),
        name="select",
    )(spread, where, own)
    rows = lax.all_to_all(outgoing, "dev", split_axis=0, concat_axis=0, tiled=True)

    half = pl.BlockSpec((2, DD, DD), lambda i: (0, 0, 0))
    other = pl.BlockSpec((2, DD, DD), lambda i: (0, 0, 1))

    def fixed(dims):
        return pl.BlockSpec(dims, lambda i: (0,) * len(dims))

    fold = pl.pallas_call(
        fold_kernel,
        grid=(1,),
        in_specs=[fixed((2, 16, DD)), half, other],
        out_specs=fixed((2, HEADS * 16, DD)),
        out_shape=shape((2, HEADS * 16, DD), BF16),
        compiler_params=params_for(32),
        cost_estimate=pl.CostEstimate(flops=2000000000, bytes_accessed=6000000, transcendentals=0),
        name="fold",
    )(head_rows, cross_out, cross_keyval)

    view_par = jnp.repeat(pair_params[0], 2, axis=0)
    points, grads = pl.pallas_call(
        decode_kernel,
        grid=(1,),
        in_specs=[
            fixed((PEERS * REFS * ROWS, DD)), fixed((384, 384)), half, half, fixed((2, HEADS * 16, DD)),
            fixed((2, 16, DD)), fixed((REFS, 256)), fixed((REFS, 13)),
        ],
        out_specs=(fixed((REFS, 4, TOK)), fixed((PEERS * REFS, 256))),
        out_shape=(shape((REFS, 4, TOK), F32), shape((PEERS * REFS, 256), F32)),
        scratch_shapes=[
            pltpu.VMEM((2, PAIRS * TOK, DD), BF16),
            pltpu.VMEM((2, PAIRS * TOK, DD), BF16),
            pltpu.VMEM((2, PAIRS * TOK, DD), BF16),
            pltpu.VMEM((2, PAIRS * TOK, DD), BF16),
            pltpu.VMEM((2, PAIRS, HEADS * 16, TOK), BF16),
            pltpu.VMEM((2, PAIRS, 8, TOK), F32),
            pltpu.VMEM((4, REFS, TOK), F32),
        ],
        compiler_params=params_for(48),
        name="decode",
    )(rows, gather_order(), cross_query, cross_keyval, fold, head_rows, my_geo, view_par)

    grads = lax.all_to_all(grads, "dev", split_axis=0, concat_axis=0, tiled=True)
    smem = pl.BlockSpec(memory_space=pltpu.SMEM)
    own_grad, square = pl.pallas_call(
        combine_kernel,
        in_specs=[smem, whole(), whole()],
        out_shape=(shape((16, 256), F32), shape((1, 128), F32)),
        name="combine",
    )(me.reshape(1), graph.reshape(1, -1), grads)
    squares = lax.all_gather(square, "grp", axis=0, tiled=True)
    count = lax.axis_size("grp") * PEERS * (2 * (TOK + 12) + 13 * PAIRS)
    new_depth, new_cameras, new_params = pl.pallas_call(
        functools.partial(update_kernel, float(count)),
        out_shape=(shape((2, TOK), F32), shape((2, 12), F32), shape((PAIRS, 13), F32)),
        name="update",
    )(squares, own_grad, depth_map[0], cameras[0], pair_params[0])
    return (
        points.reshape(1, PAIRS, 2, 4, TOK),
        new_depth[None],
        new_cameras[None],
        new_params[None],
    )


def solution(mesh):
    placed = (
        P("grp", "dev", None, None),
        P("grp", "dev"),
        P("grp", "dev", None),
        P("grp", "dev", None),
        P("grp", None, None),
        P("grp", "dev", None),
        P(),
        P(),
        P(),
        P(),
        P(),
    )
    return jax.shard_map(
        on_device,
        mesh=mesh,
        in_specs=placed,
        out_specs=(
            P("grp", "dev", None, None, None),
            P("grp", "dev", None),
            P("grp", "dev", None),
            P("grp", "dev", None),
        ),
        check_vma=False,
    )
```

```python
import functools
import math

import jax
import jax.numpy as jnp
from jax import lax
from jax.experimental import pallas as pl
from jax.experimental.pallas import tpu as pltpu
from jax.sharding import PartitionSpec as P

HEADS = 12
HD = 64
DD = 768
TOK = 192
GW = 16
PEERS = 32
REFS = 8
PAIRS = 4
SPLIT = (3, 1)
PIECE = 12
WIDE = 384
SLOTS = 32
LOW = 32

norm_eps = 1e-06
stat_eps = 1e-06
step_rate = 0.3

F32 = jnp.float32
BF16 = jnp.bfloat16
NT = (((1,), (1,)), ((), ()))
MIB = 1024 * 1024


def params_for(mib):
    return pltpu.CompilerParams(vmem_limit_bytes=mib * MIB)


def dot(left, right):
    return jnp.dot(left, right, preferred_element_type=F32)


def dot_nt(left, right):
    return lax.dot_general(left, right, NT, preferred_element_type=F32)


def one_hot(pick):
    return jnp.where(pick, 1.0, 0.0).astype(BF16)


def spread_order():
    row = lax.broadcasted_iota(jnp.int32, (8 * SLOTS, 208), 0)
    slot = row & (SLOTS - 1)
    first = (row >> 5) * PIECE + slot
    source = jnp.where(slot < PIECE, first, first + (96 - PIECE))
    source = jnp.where(slot < 2 * PIECE, source, slot + (192 - 2 * PIECE))
    source = jnp.where(slot < 2 * PIECE + 2, source, -1)
    return one_hot(source == lax.broadcasted_iota(jnp.int32, (8 * SLOTS, 208), 1))


def gather_order(images):
    size = 8 * images * PIECE
    row = lax.broadcasted_iota(jnp.int32, (size, size), 0)
    image = (row * 683) >> 16
    rest = row - image * 96
    source = (rest * 43) >> 9
    came = source * (images * PIECE) + image * PIECE + rest - source * PIECE
    return one_hot(came == lax.broadcasted_iota(jnp.int32, (size, size), 1))


def embed_kernel(tokens_hbm, weight_hbm, depth_hbm, camera_hbm, focal_hbm, out_ref,
                 tokens_ref, weight_ref, depth_ref, camera_ref, focal_ref, emb_ref, sems):
    depth_of = weight_hbm.shape[0] // 2
    parts = [pl.ds(0, depth_of), pl.ds(depth_of, depth_of)]
    copies = [
        pltpu.make_async_copy(depth_hbm, depth_ref, sems.at[0]),
        pltpu.make_async_copy(camera_hbm, camera_ref, sems.at[1]),
        pltpu.make_async_copy(focal_hbm, focal_ref, sems.at[2]),
        pltpu.make_async_copy(tokens_hbm, tokens_ref, sems.at[3]),
    ]
    copies += [
        pltpu.make_async_copy(weight_hbm.at[part], weight_ref.at[part], sems.at[4 + i])
        for i, part in enumerate(parts)
    ]
    for copy in copies:
        copy.start()
    order = spread_order()
    for copy in copies[:3]:
        copy.wait()
    blank = jnp.zeros((2, WIDE - TOK), F32)
    geo = jnp.concatenate([depth_ref[...].astype(F32), blank], axis=1)
    lane = lax.broadcasted_iota(jnp.int32, (2, WIDE), 1)
    camera = camera_ref[...].astype(F32)
    focal = focal_ref[...].astype(F32)
    upper = lax.broadcasted_iota(jnp.int32, (2, WIDE), 0) == 0
    for i in range(12):
        geo = jnp.where(lane == TOK + i, camera[:, i : i + 1], geo)
    geo = jnp.where(lane == TOK + 12, jnp.where(upper, focal[:, 0:1], focal[:, 1:2]), geo)
    geo = jnp.concatenate([geo, jnp.zeros((14, WIDE), F32)], axis=0).astype(BF16)
    copies[3].wait()
    copies[4].wait()
    first = dot(tokens_ref[:, 0:depth_of], weight_ref[0:depth_of])
    copies[5].wait()
    emb_ref[...] = (first + dot(tokens_ref[:, depth_of:], weight_ref[depth_of:])).astype(BF16)
    for part in range(4):
        cols = slice((part // 2) * WIDE, (part // 2 + 1) * WIDE)
        at = (part % 2) * 96
        rows = jnp.concatenate(
            [emb_ref[at : at + 96, cols], emb_ref[TOK + at : TOK + at + 96, cols], geo], axis=0
        )
        out_ref[part * 8 * SLOTS : (part + 1) * 8 * SLOTS] = dot(order, rows).astype(BF16)


def select_kernel(with_geo, rows_ref, where_ref, own_ref, after_ref, *rest):
    if with_geo:
        out_hbm, geo_ref, out_ref, sems = rest
    else:
        out_hbm, out_ref, sems = rest
    total = rows_ref.shape[0]
    lane = lax.broadcasted_iota(jnp.int32, (TOK, total), 1)
    copies = []
    for step in range(out_ref.shape[0] // TOK):
        at = pl.ds(step * TOK, TOK)
        pick = one_hot(where_ref[at, :][:, :1] == lane)
        out_ref[at, :] = dot(pick, rows_ref[...]).astype(BF16)
        copies.append(pltpu.make_async_copy(out_ref.at[at], out_hbm.at[at], sems.at[step]))
        copies[-1].start()
    if with_geo:
        own_lane = lax.broadcasted_iota(jnp.int32, (16, total), 1)
        own = one_hot(own_ref[...][:, :1] == own_lane)
        geo_ref[...] = dot(own, rows_ref[:, 0:256])[0:REFS]
    for copy in copies:
        copy.wait()


def fold_kernel(head_ref, out_hbm, value_hbm, fold_ref, out_ref, value_ref, sems):
    copies = []
    for view in range(2):
        copies.append(pltpu.make_async_copy(out_hbm.at[view], out_ref.at[view], sems.at[2 * view]))
        copies.append(
            pltpu.make_async_copy(value_hbm.at[view, :, pl.ds(DD, DD)], value_ref.at[view], sems.at[2 * view + 1])
        )
    for copy in copies:
        copy.start()
    lane = lax.broadcasted_iota(jnp.int32, (16, DD), 1)
    for view in range(2):
        copies[2 * view].wait()
        both = dot_nt(head_ref[view], out_ref[view])
        high = both.astype(BF16).astype(F32)
        low = (both - high).astype(BF16).astype(F32)
        pair = jnp.concatenate([high[0:8], low[0:8]], axis=0)
        left = jnp.concatenate(
            [jnp.where(lane // HD == head, pair, 0.0).astype(BF16) for head in range(HEADS)], axis=0
        )
        copies[2 * view + 1].wait()
        full = dot_nt(left, value_ref[view])
        for head in range(HEADS):
            term = full[head * 16 : head * 16 + 8] + full[head * 16 + 8 : head * 16 + 16]
            top = term.astype(BF16).astype(F32)
            rest = term - top
            fold_ref[view, head * 16 : head * 16 + 16] = jnp.concatenate([top, rest], axis=0).astype(BF16)


def view_gradients(outs, geo, par):
    token = lax.broadcasted_iota(jnp.int32, (REFS, TOK), 1)
    column = (token & (GW - 1)).astype(F32) - (GW - 1) / 2.0
    row_pos = (token >> 4).astype(F32) - (TOK // GW - 1) / 2.0
    depth = geo[:, 0:TOK]
    cam = [geo[:, TOK + i : TOK + i + 1] for i in range(12)]
    focal = geo[:, TOK + 12 : TOK + 13]
    ray = [column / focal, row_pos / focal, jnp.ones_like(column)]
    cam_points = [depth * ray[0], depth * ray[1], depth]
    scale = par[:, 0:1]
    mat = [par[:, 1 + i : 2 + i] for i in range(9)]
    shift = [par[:, 10 + i : 11 + i] for i in range(3)]
    points = outs[:3]
    confidence = outs[3]
    fitted, weighted, ray_image = [], [], []
    for r in range(3):
        world = cam[3 * r] * cam_points[0] + cam[3 * r + 1] * cam_points[1] + cam[3 * r + 2] * cam_points[2]
        world = world + cam[9 + r]
        fit = mat[3 * r] * points[0] + mat[3 * r + 1] * points[1] + mat[3 * r + 2] * points[2] + shift[r]
        fitted.append(fit)
        weighted.append((2.0 * confidence) * (world - scale * fit))
        ray_image.append(cam[3 * r] * ray[0] + cam[3 * r + 1] * ray[1] + cam[3 * r + 2])
    grad_depth = weighted[0] * ray_image[0] + weighted[1] * ray_image[1] + weighted[2] * ray_image[2]

    def total(x):
        return jnp.sum(x, axis=1, keepdims=True)

    sums = [total(w) for w in weighted]
    entries = [total(weighted[r] * cam_points[c]) for r in range(3) for c in range(3)] + sums
    entries.append(-total(weighted[0] * fitted[0] + weighted[1] * fitted[1] + weighted[2] * fitted[2]))
    entries += [-scale * total(weighted[r] * points[c]) for r in range(3) for c in range(3)]
    entries += [-scale * s for s in sums]
    lane = lax.broadcasted_iota(jnp.int32, (REFS, 64), 1)
    tail = jnp.zeros((REFS, 64), F32)
    for i, entry in enumerate(entries):
        high = entry.astype(BF16).astype(F32)
        tail = jnp.where(lane == i, high, jnp.where(lane == LOW + i, entry - high, tail))
    return grad_depth, tail


def decode_kernel(last, pairs, rows_ref, query_hbm, key_hbm, fold_ref, head_ref, *rest):
    if last:
        geo_ref, par_ref, past_ref, points_ref, grad_ref, o_ref, *rest = rest
    else:
        o_ref, *rest = rest
    query_ref, key_ref, x_ref, n_ref, q_ref, k_ref, u_ref, e_ref, sems = rest
    copies = []
    for view in range(2):
        copies.append(pltpu.make_async_copy(query_hbm.at[view], query_ref.at[view], sems.at[2 * view]))
        copies.append(
            pltpu.make_async_copy(key_hbm.at[view, :, pl.ds(0, DD)], key_ref.at[view], sems.at[2 * view + 1])
        )
    for copy in copies:
        copy.start()
    order = gather_order(2 * pairs)
    size = 8 * 2 * pairs * PIECE
    for part in range(4):
        mixed = dot(order, rows_ref[part * size : (part + 1) * size]).astype(BF16)
        cols = slice((part // 2) * WIDE, (part // 2 + 1) * WIDE)
        for image in range(2 * pairs):
            at = (image // 2) * TOK + (part % 2) * 96
            x_ref[image % 2, at : at + 96, cols] = mixed[image * 96 : image * 96 + 96]

    for slot in range(2):
        for pair in range(pairs):
            at = pl.ds(pair * TOK, TOK)
            wide = x_ref[slot, at, :].astype(F32)
            centred = wide - jnp.mean(wide, axis=-1, keepdims=True)
            spread = jnp.mean(centred * centred, axis=-1, keepdims=True)
            n_ref[slot, at, :] = (centred * lax.rsqrt(spread + norm_eps)).astype(BF16)

    ones_row = jnp.where(lax.broadcasted_iota(jnp.int32, (8, TOK), 0) == 4, 1.0, 0.0)
    for view in range(2):
        copies[2 * view].wait()
        q_ref[view] = dot(n_ref[view], query_ref[view]).astype(BF16)
        copies[2 * view + 1].wait()
        k_ref[view] = dot(n_ref[1 - view], key_ref[view]).astype(BF16)
        for pair in range(pairs):
            at = pl.ds(pair * TOK, TOK)
            value = dot_nt(fold_ref[view], n_ref[1 - view, at, :])
            for head in range(HEADS):
                term = value[head * 16 : head * 16 + 8] + value[head * 16 + 8 : head * 16 + 16] + ones_row
                u_ref[view, pair, head * 16 : head * 16 + 16] = jnp.concatenate(
                    [term, jnp.zeros_like(term)], axis=0
                ).astype(BF16)
            e_ref[view, pair] = dot_nt(head_ref[view], x_ref[view, at, :])[0:8]

    upper = lax.broadcasted_iota(jnp.int32, (TOK, 2 * HD), 1) >= HD
    factor = math.log2(math.e) / math.sqrt(HD)
    for view in range(2):
        @pl.loop(0, pairs)
        def _(pair):
            at = pl.ds(pl.multiple_of(pair * TOK, TOK), TOK)
            acc = e_ref[view, pair]
            for two in range(HEADS // 2):
                cols = slice(two * 2 * HD, (two + 1) * 2 * HD)
                keys = k_ref[view, at, cols]
                queries = q_ref[view, at, cols]
                for half in range(2):
                    head = 2 * two + half
                    part = jnp.where(upper if half else jnp.logical_not(upper), queries, jnp.zeros_like(queries))
                    scores = dot_nt(keys, part)
                    top = jnp.max(scores, axis=0, keepdims=True)
                    probs = jnp.exp2((scores - top) * factor).astype(BF16)
                    mixed = dot(u_ref[view, pair, head * 16 : head * 16 + 16], probs)[0:8]
                    acc = acc + mixed * (1.0 / mixed[4:5])
            sub = lax.broadcasted_iota(jnp.int32, (8, TOK), 0)
            acc = jnp.where(sub == 3, 1.0 + jnp.exp(acc), acc)
            for c in range(4):
                o_ref[c, pl.ds(2 * pair + view, 1), :] = acc[c : c + 1]

    if last:
        outs = [jnp.concatenate([past_ref[c], o_ref[c]], axis=0) for c in range(4)]
        for c in range(4):
            for view in range(REFS):
                points_ref[view, c : c + 1] = outs[c][view : view + 1]
        grad_depth, tail = view_gradients(outs, geo_ref[...], par_ref[...])
        both = jnp.concatenate([grad_depth, tail], axis=1)
        twice = jnp.concatenate([both, both], axis=0).astype(BF16)
        for peer in range(0, PEERS, 2):
            grad_ref[peer * REFS : (peer + 2) * REFS] = twice


def combine_kernel(me_ref, graph_ref, grad_ref, own_ref, square_ref):
    refs = PEERS * REFS
    me = me_ref[0]
    graph = graph_ref[...]
    grads = grad_ref[...]

    def summed(pick):
        sums = dot(jnp.where(pick, 1.0, 0.0).astype(BF16), grads)
        lane = lax.broadcasted_iota(jnp.int32, sums.shape, 1)
        return jnp.where(lane < TOK, sums, sums + pltpu.roll(sums, 256 - LOW, 1)), lane

    image = lax.broadcasted_iota(jnp.int32, (2 * PEERS, refs), 0)
    image_sum, image_lane = summed(graph == image)
    pair = lax.broadcasted_iota(jnp.int32, (refs // 2, refs), 0)
    view = lax.broadcasted_iota(jnp.int32, (refs // 2, refs), 1)
    pair_sum, pair_lane = summed((view >> 1) == pair)
    image_sq = jnp.where(image_lane < TOK + 12, image_sum * image_sum, 0.0)
    pair_sq = jnp.where((pair_lane >= TOK + 12) & (pair_lane < TOK + 25), pair_sum * pair_sum, 0.0)
    square_ref[...] = jnp.full(square_ref.shape, jnp.sum(image_sq) + jnp.sum(pair_sq), F32)
    row = lax.broadcasted_iota(jnp.int32, (16, refs), 0)
    ref = lax.broadcasted_iota(jnp.int32, (16, refs), 1)
    own_image = (row < 2) & (graph == 2 * me + row)
    own_pair = (row >= 8) & (row < 8 + PAIRS) & ((ref >> 1) == PAIRS * me + row - 8)
    own_ref[...] = summed(own_image | own_pair)[0]


def update_kernel(count, square_ref, own_ref, depth_ref, camera_ref, par_ref, depth_out, camera_out, par_out):
    total = jnp.sum(square_ref[...], axis=0, keepdims=True)[:, 0:1]
    step = step_rate / jnp.sqrt(total / count + stat_eps)
    depth_out[...] = depth_ref[...].astype(F32) - step * own_ref[0:2, 0:TOK]
    camera_out[...] = camera_ref[...].astype(F32) - step * own_ref[0:2, TOK : TOK + 12]
    par_out[...] = par_ref[...] - step * own_ref[8 : 8 + PAIRS, TOK + 12 : TOK + 25]


def shape(dims, kind):
    return jax.ShapeDtypeStruct(dims, kind)


def hbm(x):
    return pltpu.with_memory_space_constraint(x, pltpu.HBM)


def on_device(
    enc_tokens, focal_len, depth_map, cameras, pair_graph, pair_params,
    embed_weight, cross_query, cross_keyval, cross_out, point_heads,
):
    me = lax.axis_index("dev")
    groups = lax.axis_size("grp")
    inside = pl.BlockSpec(memory_space=pltpu.VMEM)
    outside = pl.BlockSpec(memory_space=pltpu.HBM)
    scalar = pl.BlockSpec(memory_space=pltpu.SMEM)

    def exchange(x, axis):
        return lax.all_to_all(x, axis, split_axis=0, concat_axis=0, tiled=True)

    tokens = enc_tokens[0].reshape(2 * TOK, -1)
    message = pl.pallas_call(
        embed_kernel,
        in_specs=[outside] * 5,
        out_specs=inside,
        out_shape=shape((PEERS * SLOTS, WIDE), BF16),
        scratch_shapes=[
            pltpu.VMEM(tokens.shape, BF16),
            pltpu.VMEM(embed_weight.shape, BF16),
            pltpu.VMEM((2, TOK), BF16),
            pltpu.VMEM((2, 12), BF16),
            pltpu.VMEM((1, 2), BF16),
            pltpu.VMEM((2 * TOK, DD), BF16),
            pltpu.SemaphoreType.DMA((6,)),
        ],
        compiler_params=params_for(24),
        name="embed",
    )(hbm(tokens), hbm(embed_weight), hbm(depth_map[0]), hbm(cameras[0]), hbm(focal_len))
    spread = exchange(message, "dev")

    head_rows = jnp.pad(jnp.swapaxes(point_heads, 1, 2), ((0, 0), (0, 12), (0, 0)))
    fold = pl.pallas_call(
        fold_kernel,
        in_specs=[inside, outside, outside],
        out_specs=inside,
        out_shape=shape((2, HEADS * 16, DD), BF16),
        scratch_shapes=[
            pltpu.VMEM((2, DD, DD), BF16),
            pltpu.VMEM((2, DD, DD), BF16),
            pltpu.SemaphoreType.DMA((4,)),
        ],
        compiler_params=params_for(20),
        cost_estimate=pl.CostEstimate(flops=2000000000, bytes_accessed=6000000, transcendentals=0),
        name="fold",
    )(head_rows, hbm(cross_out), hbm(cross_keyval))

    graph = pair_graph[0].reshape(PEERS * REFS)
    first = (graph // 2) * SLOTS + (graph % 2) * PIECE
    where = first.reshape(PEERS, REFS, 1) + jnp.arange(PIECE, dtype=jnp.int32)
    mine = lax.dynamic_slice_in_dim(graph, me * REFS, REFS)
    own = jnp.pad((mine // 2) * SLOTS + 2 * PIECE + mine % 2, (0, 8))[:, None]
    rows = []
    done = 0
    for pairs in SPLIT:
        count = PEERS * 2 * pairs * PIECE
        last = done + pairs == PAIRS
        moved = shape((count, WIDE), BF16)
        outgoing = pl.pallas_call(
            functools.partial(select_kernel, last),
            in_specs=[inside] * 3 + [pl.BlockSpec(memory_space=pl.ANY)],
            out_specs=(outside, inside) if last else outside,
            out_shape=(moved, shape((REFS, 256), F32)) if last else moved,
            scratch_shapes=[pltpu.VMEM((count, WIDE), BF16), pltpu.SemaphoreType.DMA((count // TOK,))],
            compiler_params=params_for(20),
            cost_estimate=pl.CostEstimate(flops=count * 800000, bytes_accessed=4 * count * WIDE, transcendentals=0),
            name="select",
        )(spread, where[:, 2 * done : 2 * (done + pairs)].reshape(count, 1), own, fold)
        if last:
            outgoing, my_geo = outgoing
        rows.append(exchange(outgoing, "dev"))
        done += pairs

    view_par = jnp.repeat(pair_params[0], 2, axis=0)
    for part, pairs in enumerate(SPLIT):
        last = part == len(SPLIT) - 1
        weights = pltpu.VMEM((2, DD, DD), BF16)
        tokens_of = pltpu.VMEM((2, pairs * TOK, DD), BF16)
        scratch = [weights] * 2 + [tokens_of] * 4
        scratch += [pltpu.VMEM((2, pairs, HEADS * 16, TOK), BF16), pltpu.VMEM((2, pairs, 8, TOK), F32)]
        scratch.append(pltpu.SemaphoreType.DMA((4,)))
        if last:
            extra = (my_geo, view_par, past)
            outs = (shape((REFS, 4, TOK), F32), shape((PEERS * REFS, 256), BF16))
            scratch = [pltpu.VMEM((4, 2 * pairs, TOK), F32)] + scratch
        else:
            extra = ()
            outs = (shape((4, 2 * pairs, TOK), F32),)
        past = pl.pallas_call(
            functools.partial(decode_kernel, last, pairs),
            in_specs=[inside] + [outside] * 2 + [inside] * (2 + len(extra)),
            out_specs=(inside,) * len(outs),
            out_shape=outs,
            scratch_shapes=scratch,
            compiler_params=params_for(28),
            cost_estimate=pl.CostEstimate(flops=4000000000 * pairs, bytes_accessed=8000000, transcendentals=0),
            name="decode",
        )(rows[part], hbm(cross_query), hbm(cross_keyval), fold, head_rows, *extra)
        past = past if last else past[0]
    points, grads = past

    own_grad, square = pl.pallas_call(
        combine_kernel,
        in_specs=[scalar, inside, inside],
        out_shape=(shape((16, 256), F32), shape((groups, 128), F32)),
        compiler_params=params_for(16),
        name="combine",
    )(me.reshape(1), graph.reshape(1, -1), exchange(grads, "dev"))
    total = groups * PEERS * (2 * (TOK + 12) + 13 * PAIRS)
    new_depth, new_cameras, new_params = pl.pallas_call(
        functools.partial(update_kernel, float(total)),
        out_shape=(shape((2, TOK), F32), shape((2, 12), F32), shape((PAIRS, 13), F32)),
        compiler_params=params_for(16),
        name="update",
    )(exchange(square, "grp"), own_grad, depth_map[0], cameras[0], pair_params[0])
    return (
        points.reshape(1, PAIRS, 2, 4, TOK),
        new_depth[None],
        new_cameras[None],
        new_params[None],
    )


def solution(mesh):
    placed = (
        P("grp", "dev", None, None),
        P("grp", "dev"),
        P("grp", "dev", None),
        P("grp", "dev", None),
        P("grp", None, None),
        P("grp", "dev", None),
        P(),
        P(),
        P(),
        P(),
        P(),
    )
    return jax.shard_map(
        on_device,
        mesh=mesh,
        in_specs=placed,
        out_specs=(
            P("grp", "dev", None, None, None),
            P("grp", "dev", None),
            P("grp", "dev", None),
            P("grp", "dev", None),
        ),
        check_vma=False,
    )
```

```python
import functools
import math

import jax
import jax.numpy as jnp
from jax import lax
from jax.experimental import pallas as pl
from jax.experimental.pallas import tpu as pltpu
from jax.sharding import PartitionSpec as P

HEADS = 12
HD = 64
DD = 768
TOK = 192
GW = 16
PEERS = 32
REFS = 8
PAIRS = 4
SPLIT = (3, 1)
PIECE = 12
WIDE = 384
GROUPS = 3
LOW = 32

norm_eps = 1e-06
stat_eps = 1e-06
step_rate = 0.3

F32 = jnp.float32
BF16 = jnp.bfloat16
NT = (((1,), (1,)), ((), ()))
MIB = 1024 * 1024


def params_for(mib):
    return pltpu.CompilerParams(vmem_limit_bytes=mib * MIB)


def dot(left, right):
    return jnp.dot(left, right, preferred_element_type=F32)


def dot_nt(left, right):
    return lax.dot_general(left, right, NT, preferred_element_type=F32)


def one_hot(pick):
    return jnp.where(pick, 1.0, 0.0).astype(BF16)


def spread_order(group):
    row = lax.broadcasted_iota(jnp.int32, (64, TOK), 0)
    slot = group * 8 + (row & 7)
    first = (row >> 3) * PIECE + slot
    source = jnp.where(slot < PIECE, first, first + (96 - PIECE))
    return one_hot(source == lax.broadcasted_iota(jnp.int32, (64, TOK), 1))


def gather_order(images):
    size = 8 * images * PIECE
    row = lax.broadcasted_iota(jnp.int32, (size, size), 0)
    image = (row * 683) >> 16
    rest = row - image * 96
    source = (rest * 43) >> 9
    came = source * (images * PIECE) + image * PIECE + rest - source * PIECE
    return one_hot(came == lax.broadcasted_iota(jnp.int32, (size, size), 1))


def embed_kernel(tokens_hbm, weight_hbm, depth_hbm, camera_hbm, focal_hbm, out_ref,
                 tokens_ref, weight_ref, depth_ref, camera_ref, focal_ref, emb_ref, sems):
    depth_of = weight_hbm.shape[0] // 2
    parts = [pl.ds(0, depth_of), pl.ds(depth_of, depth_of)]
    copies = [
        pltpu.make_async_copy(depth_hbm, depth_ref, sems.at[0]),
        pltpu.make_async_copy(camera_hbm, camera_ref, sems.at[1]),
        pltpu.make_async_copy(focal_hbm, focal_ref, sems.at[2]),
        pltpu.make_async_copy(tokens_hbm, tokens_ref, sems.at[3]),
    ]
    copies += [
        pltpu.make_async_copy(weight_hbm.at[part], weight_ref.at[part], sems.at[4 + i])
        for i, part in enumerate(parts)
    ]
    for copy in copies:
        copy.start()
    orders = [spread_order(group) for group in range(GROUPS)]
    for copy in copies[:3]:
        copy.wait()
    depth = depth_ref[...].astype(F32)
    tail = jnp.concatenate([depth[:, 128:TOK], jnp.zeros((2, 64), F32)], axis=1)
    lane = lax.broadcasted_iota(jnp.int32, (2, 128), 1)
    camera = camera_ref[...].astype(F32)
    focal = focal_ref[...].astype(F32)
    upper = lax.broadcasted_iota(jnp.int32, (2, 128), 0) == 0
    for i in range(12):
        tail = jnp.where(lane == 64 + i, camera[:, i : i + 1], tail)
    tail = jnp.where(lane == 76, jnp.where(upper, focal[:, 0:1], focal[:, 1:2]), tail)
    head = depth[:, 0:128]
    geo = jnp.concatenate([head[0:1], tail[0:1], head[1:2], tail[1:2], jnp.zeros((4, 128), F32)], axis=0)
    geo = jnp.concatenate([geo, geo], axis=0).astype(BF16)
    for two in range(PEERS // 2):
        out_ref[two * 16 : two * 16 + 16, GROUPS * WIDE :] = geo
    copies[3].wait()
    copies[4].wait()
    first = dot(tokens_ref[:, 0:depth_of], weight_ref[0:depth_of])
    copies[5].wait()
    emb_ref[...] = (first + dot(tokens_ref[:, depth_of:], weight_ref[depth_of:])).astype(BF16)
    for part in range(4):
        cols = slice((part // 2) * WIDE, (part // 2 + 1) * WIDE)
        at = (part % 2) * 96
        rows = jnp.concatenate([emb_ref[at : at + 96, cols], emb_ref[TOK + at : TOK + at + 96, cols]], axis=0)
        for group in range(GROUPS):
            out_ref[part * 64 : part * 64 + 64, group * WIDE : (group + 1) * WIDE] = dot(orders[group], rows).astype(BF16)


def select_kernel(with_geo, rows_ref, where_ref, own_ref, after_ref, *rest):
    if with_geo:
        out_hbm, geo_ref, out_ref, sems = rest
    else:
        out_hbm, out_ref, sems = rest
    total = rows_ref.shape[0]
    rows = jnp.concatenate([rows_ref[:, group * WIDE : (group + 1) * WIDE] for group in range(GROUPS)], axis=0)
    lane = lax.broadcasted_iota(jnp.int32, (TOK, GROUPS * total), 1)
    copies = []
    for step in range(out_ref.shape[0] // TOK):
        at = pl.ds(step * TOK, TOK)
        pick = one_hot(where_ref[at, :][:, :1] == lane)
        out_ref[at, :] = dot(pick, rows).astype(BF16)
        copies.append(pltpu.make_async_copy(out_ref.at[at], out_hbm.at[at], sems.at[step]))
        copies[-1].start()
    if with_geo:
        own_lane = lax.broadcasted_iota(jnp.int32, (16, total), 1)
        own = own_ref[...][:, :1]
        for half in range(2):
            found = dot(one_hot(own + half == own_lane), rows_ref[:, GROUPS * WIDE :])
            geo_ref[:, half * 128 : half * 128 + 128] = found[0:REFS]
    for copy in copies:
        copy.wait()


def fold_kernel(head_ref, out_hbm, value_hbm, fold_ref, out_ref, value_ref, sems):
    copies = []
    for view in range(2):
        copies.append(pltpu.make_async_copy(out_hbm.at[view], out_ref.at[view], sems.at[2 * view]))
        copies.append(
            pltpu.make_async_copy(value_hbm.at[view, :, pl.ds(DD, DD)], value_ref.at[view], sems.at[2 * view + 1])
        )
    for copy in copies:
        copy.start()
    lane = lax.broadcasted_iota(jnp.int32, (16, DD), 1)
    for view in range(2):
        copies[2 * view].wait()
        both = dot_nt(head_ref[view], out_ref[view])
        high = both.astype(BF16).astype(F32)
        low = (both - high).astype(BF16).astype(F32)
        pair = jnp.concatenate([high[0:8], low[0:8]], axis=0)
        left = jnp.concatenate(
            [jnp.where(lane // HD == head, pair, 0.0).astype(BF16) for head in range(HEADS)], axis=0
        )
        copies[2 * view + 1].wait()
        full = dot_nt(left, value_ref[view])
        for head in range(HEADS):
            term = full[head * 16 : head * 16 + 8] + full[head * 16 + 8 : head * 16 + 16]
            top = term.astype(BF16).astype(F32)
            rest = term - top
            fold_ref[view, head * 16 : head * 16 + 16] = jnp.concatenate([top, rest], axis=0).astype(BF16)


def view_gradients(outs, geo, par):
    token = lax.broadcasted_iota(jnp.int32, (REFS, TOK), 1)
    column = (token & (GW - 1)).astype(F32) - (GW - 1) / 2.0
    row_pos = (token >> 4).astype(F32) - (TOK // GW - 1) / 2.0
    depth = geo[:, 0:TOK]
    cam = [geo[:, TOK + i : TOK + i + 1] for i in range(12)]
    focal = geo[:, TOK + 12 : TOK + 13]
    ray = [column / focal, row_pos / focal, jnp.ones_like(column)]
    cam_points = [depth * ray[0], depth * ray[1], depth]
    scale = par[:, 0:1]
    mat = [par[:, 1 + i : 2 + i] for i in range(9)]
    shift = [par[:, 10 + i : 11 + i] for i in range(3)]
    points = outs[:3]
    confidence = outs[3]
    fitted, weighted, ray_image = [], [], []
    for r in range(3):
        world = cam[3 * r] * cam_points[0] + cam[3 * r + 1] * cam_points[1] + cam[3 * r + 2] * cam_points[2]
        world = world + cam[9 + r]
        fit = mat[3 * r] * points[0] + mat[3 * r + 1] * points[1] + mat[3 * r + 2] * points[2] + shift[r]
        fitted.append(fit)
        weighted.append((2.0 * confidence) * (world - scale * fit))
        ray_image.append(cam[3 * r] * ray[0] + cam[3 * r + 1] * ray[1] + cam[3 * r + 2])
    grad_depth = weighted[0] * ray_image[0] + weighted[1] * ray_image[1] + weighted[2] * ray_image[2]

    def total(x):
        return jnp.sum(x, axis=1, keepdims=True)

    sums = [total(w) for w in weighted]
    entries = [total(weighted[r] * cam_points[c]) for r in range(3) for c in range(3)] + sums
    entries.append(-total(weighted[0] * fitted[0] + weighted[1] * fitted[1] + weighted[2] * fitted[2]))
    entries += [-scale * total(weighted[r] * points[c]) for r in range(3) for c in range(3)]
    entries += [-scale * s for s in sums]
    lane = lax.broadcasted_iota(jnp.int32, (REFS, 64), 1)
    tail = jnp.zeros((REFS, 64), F32)
    for i, entry in enumerate(entries):
        high = entry.astype(BF16).astype(F32)
        tail = jnp.where(lane == i, high, jnp.where(lane == LOW + i, entry - high, tail))
    return grad_depth, tail


def decode_kernel(last, pairs, rows_ref, query_hbm, key_hbm, fold_ref, head_ref, *rest):
    if last:
        past_ref = None
        if pairs < PAIRS:
            past_ref, *rest = rest
        geo_ref, par_ref, points_ref, grad_ref, o_ref, *rest = rest
    else:
        o_ref, *rest = rest
    query_ref, key_ref, x_ref, n_ref, q_ref, k_ref, u_ref, e_ref, sems = rest
    copies = []
    for view in range(2):
        copies.append(pltpu.make_async_copy(query_hbm.at[view], query_ref.at[view], sems.at[2 * view]))
        copies.append(
            pltpu.make_async_copy(key_hbm.at[view, :, pl.ds(0, DD)], key_ref.at[view], sems.at[2 * view + 1])
        )
    for copy in copies:
        copy.start()
    order = gather_order(2 * pairs)
    size = 8 * 2 * pairs * PIECE
    for part in range(4):
        mixed = dot(order, rows_ref[part * size : (part + 1) * size]).astype(BF16)
        cols = slice((part // 2) * WIDE, (part // 2 + 1) * WIDE)
        for image in range(2 * pairs):
            at = (image // 2) * TOK + (part % 2) * 96
            x_ref[image % 2, at : at + 96, cols] = mixed[image * 96 : image * 96 + 96]

    for slot in range(2):
        for pair in range(pairs):
            at = pl.ds(pair * TOK, TOK)
            wide = x_ref[slot, at, :].astype(F32)
            centred = wide - jnp.mean(wide, axis=-1, keepdims=True)
            spread = jnp.mean(centred * centred, axis=-1, keepdims=True)
            n_ref[slot, at, :] = (centred * lax.rsqrt(spread + norm_eps)).astype(BF16)

    ones_row = jnp.where(lax.broadcasted_iota(jnp.int32, (8, TOK), 0) == 4, 1.0, 0.0)
    for view in range(2):
        copies[2 * view].wait()
        q_ref[view] = dot(n_ref[view], query_ref[view]).astype(BF16)
        copies[2 * view + 1].wait()
        k_ref[view] = dot(n_ref[1 - view], key_ref[view]).astype(BF16)
        for pair in range(pairs):
            at = pl.ds(pair * TOK, TOK)
            value = dot_nt(fold_ref[view], n_ref[1 - view, at, :])
            for head in range(HEADS):
                term = value[head * 16 : head * 16 + 8] + value[head * 16 + 8 : head * 16 + 16] + ones_row
                u_ref[view, pair, head * 16 : head * 16 + 16] = jnp.concatenate(
                    [term, jnp.zeros_like(term)], axis=0
                ).astype(BF16)
            e_ref[view, pair] = dot_nt(head_ref[view], x_ref[view, at, :])[0:8]

    four_of = lax.broadcasted_iota(jnp.int32, (TOK, 4 * HD), 1) // HD
    block_of = lax.broadcasted_iota(jnp.int32, (8, 4 * TOK), 1) // TOK
    factor = math.log2(math.e) / math.sqrt(HD)
    for view in range(2):
        @pl.loop(0, pairs, unroll=True)
        def _(pair):
            at = pl.ds(pl.multiple_of(pair * TOK, TOK), TOK)
            acc = jnp.zeros((8, 4 * TOK), F32)
            for four in range(HEADS // 4):
                cols = slice(four * 4 * HD, (four + 1) * 4 * HD)
                keys = k_ref[view, at, cols]
                queries = q_ref[view, at, cols]
                blocks = jnp.concatenate(
                    [jnp.where(four_of == head, queries, jnp.zeros_like(queries)) for head in range(4)], axis=0
                )
                scores = dot_nt(keys, blocks)
                top = jnp.max(scores, axis=0, keepdims=True)
                probs = jnp.exp2((scores - top) * factor).astype(BF16)
                mixed = dot(u_ref[view, pair, four * 64 : four * 64 + 64], probs)
                own = mixed[0:8]
                for head in range(1, 4):
                    own = jnp.where(block_of == head, mixed[head * 16 : head * 16 + 8], own)
                acc = acc + own * (1.0 / own[4:5])
            acc = acc[:, 0:TOK] + acc[:, TOK : 2 * TOK] + acc[:, 2 * TOK : 3 * TOK] + acc[:, 3 * TOK :]
            acc = acc + e_ref[view, pair]
            sub = lax.broadcasted_iota(jnp.int32, (8, TOK), 0)
            acc = jnp.where(sub == 3, 1.0 + jnp.exp(acc), acc)
            for c in range(4):
                o_ref[c, pl.ds(2 * pair + view, 1), :] = acc[c : c + 1]

    if last:
        outs = [o_ref[c] if past_ref is None else jnp.concatenate([past_ref[c], o_ref[c]], axis=0) for c in range(4)]
        for c in range(4):
            for view in range(REFS):
                points_ref[view, c : c + 1] = outs[c][view : view + 1]
        grad_depth, tail = view_gradients(outs, geo_ref[...], par_ref[...])
        both = jnp.concatenate([grad_depth, tail], axis=1)
        twice = jnp.concatenate([both, both], axis=0).astype(BF16)
        for peer in range(0, PEERS, 2):
            grad_ref[peer * REFS : (peer + 2) * REFS] = twice


def combine_kernel(me_ref, graph_ref, grad_ref, own_ref, square_ref):
    refs = PEERS * REFS
    me = me_ref[0]
    graph = graph_ref[...]
    grads = grad_ref[...]

    def summed(pick):
        sums = dot(jnp.where(pick, 1.0, 0.0).astype(BF16), grads)
        lane = lax.broadcasted_iota(jnp.int32, sums.shape, 1)
        return jnp.where(lane < TOK, sums, sums + pltpu.roll(sums, 256 - LOW, 1)), lane

    image = lax.broadcasted_iota(jnp.int32, (2 * PEERS, refs), 0)
    image_sum, image_lane = summed(graph == image)
    pair = lax.broadcasted_iota(jnp.int32, (refs // 2, refs), 0)
    view = lax.broadcasted_iota(jnp.int32, (refs // 2, refs), 1)
    pair_sum, pair_lane = summed((view >> 1) == pair)
    image_sq = jnp.where(image_lane < TOK + 12, image_sum * image_sum, 0.0)
    pair_sq = jnp.where((pair_lane >= TOK + 12) & (pair_lane < TOK + 25), pair_sum * pair_sum, 0.0)
    square_ref[...] = jnp.full(square_ref.shape, jnp.sum(image_sq) + jnp.sum(pair_sq), F32)
    row = lax.broadcasted_iota(jnp.int32, (16, refs), 0)
    ref = lax.broadcasted_iota(jnp.int32, (16, refs), 1)
    own_image = (row < 2) & (graph == 2 * me + row)
    own_pair = (row >= 8) & (row < 8 + PAIRS) & ((ref >> 1) == PAIRS * me + row - 8)
    own_ref[...] = summed(own_image | own_pair)[0]


def update_kernel(count, square_ref, own_ref, depth_ref, camera_ref, par_ref, depth_out, camera_out, par_out):
    total = jnp.sum(square_ref[...], axis=0, keepdims=True)[:, 0:1]
    step = step_rate / jnp.sqrt(total / count + stat_eps)
    depth_out[...] = depth_ref[...].astype(F32) - step * own_ref[0:2, 0:TOK]
    camera_out[...] = camera_ref[...].astype(F32) - step * own_ref[0:2, TOK : TOK + 12]
    par_out[...] = par_ref[...] - step * own_ref[8 : 8 + PAIRS, TOK + 12 : TOK + 25]


def shape(dims, kind):
    return jax.ShapeDtypeStruct(dims, kind)


def hbm(x):
    return pltpu.with_memory_space_constraint(x, pltpu.HBM)


def on_device(
    enc_tokens, focal_len, depth_map, cameras, pair_graph, pair_params,
    embed_weight, cross_query, cross_keyval, cross_out, point_heads,
):
    me = lax.axis_index("dev")
    groups = lax.axis_size("grp")
    inside = pl.BlockSpec(memory_space=pltpu.VMEM)
    outside = pl.BlockSpec(memory_space=pltpu.HBM)
    scalar = pl.BlockSpec(memory_space=pltpu.SMEM)

    def exchange(x, axis):
        return lax.all_to_all(x, axis, split_axis=0, concat_axis=0, tiled=True)

    tokens = enc_tokens[0].reshape(2 * TOK, -1)
    message = pl.pallas_call(
        embed_kernel,
        in_specs=[outside] * 5,
        out_specs=inside,
        out_shape=shape((PEERS * 8, GROUPS * WIDE + 128), BF16),
        scratch_shapes=[
            pltpu.VMEM(tokens.shape, BF16),
            pltpu.VMEM(embed_weight.shape, BF16),
            pltpu.VMEM((2, TOK), BF16),
            pltpu.VMEM((2, 12), BF16),
            pltpu.VMEM((1, 2), BF16),
            pltpu.VMEM((2 * TOK, DD), BF16),
            pltpu.SemaphoreType.DMA((6,)),
        ],
        compiler_params=params_for(24),
        name="embed",
    )(hbm(tokens), hbm(embed_weight), hbm(depth_map[0]), hbm(cameras[0]), hbm(focal_len))
    spread = exchange(message, "dev")

    head_rows = jnp.pad(jnp.swapaxes(point_heads, 1, 2), ((0, 0), (0, 12), (0, 0)))
    fold = pl.pallas_call(
        fold_kernel,
        in_specs=[inside, outside, outside],
        out_specs=inside,
        out_shape=shape((2, HEADS * 16, DD), BF16),
        scratch_shapes=[
            pltpu.VMEM((2, DD, DD), BF16),
            pltpu.VMEM((2, DD, DD), BF16),
            pltpu.SemaphoreType.DMA((4,)),
        ],
        compiler_params=params_for(20),
        cost_estimate=pl.CostEstimate(flops=2000000000, bytes_accessed=6000000, transcendentals=0),
        name="fold",
    )(head_rows, hbm(cross_out), hbm(cross_keyval))

    graph = pair_graph[0].reshape(PEERS * REFS)
    slot = (graph % 2)[:, None] * PIECE + jnp.arange(PIECE, dtype=jnp.int32)
    where = (slot // 8) * (PEERS * 8) + (graph // 2)[:, None] * 8 + slot % 8
    where = where.reshape(PEERS, REFS, PIECE)
    mine = lax.dynamic_slice_in_dim(graph, me * REFS, REFS)
    own = jnp.pad((mine // 2) * 8 + 2 * (mine % 2), (0, 8))[:, None]
    rows = []
    done = 0
    for pairs in SPLIT:
        count = PEERS * 2 * pairs * PIECE
        last = done + pairs == PAIRS
        moved = shape((count, WIDE), BF16)
        outgoing = pl.pallas_call(
            functools.partial(select_kernel, last),
            in_specs=[inside] * 3 + [pl.BlockSpec(memory_space=pl.ANY)],
            out_specs=(outside, inside) if last else outside,
            out_shape=(moved, shape((REFS, 256), F32)) if last else moved,
            scratch_shapes=[pltpu.VMEM((count, WIDE), BF16), pltpu.SemaphoreType.DMA((count // TOK,))],
            compiler_params=params_for(20),
            cost_estimate=pl.CostEstimate(flops=count * 800000, bytes_accessed=4 * count * WIDE, transcendentals=0),
            name="select",
        )(spread, where[:, 2 * done : 2 * (done + pairs)].reshape(count, 1), own, fold)
        if last:
            outgoing, my_geo = outgoing
        rows.append(exchange(outgoing, "dev"))
        done += pairs

    view_par = jnp.repeat(pair_params[0], 2, axis=0)
    past = ()
    for part, pairs in enumerate(SPLIT):
        last = part == len(SPLIT) - 1
        weights = pltpu.VMEM((2, DD, DD), BF16)
        tokens_of = pltpu.VMEM((2, pairs * TOK, DD), BF16)
        scratch = [weights] * 2 + [tokens_of] * 4
        scratch += [pltpu.VMEM((2, pairs, HEADS * 16, TOK), BF16), pltpu.VMEM((2, pairs, 8, TOK), F32)]
        scratch.append(pltpu.SemaphoreType.DMA((4,)))
        if last:
            extra = (*past, my_geo, view_par)
            outs = (shape((REFS, 4, TOK), F32), shape((PEERS * REFS, 256), BF16))
            scratch = [pltpu.VMEM((4, 2 * pairs, TOK), F32)] + scratch
        else:
            extra = ()
            outs = (shape((4, 2 * pairs, TOK), F32),)
        past = pl.pallas_call(
            functools.partial(decode_kernel, last, pairs),
            in_specs=[inside] + [outside] * 2 + [inside] * (2 + len(extra)),
            out_specs=(inside,) * len(outs),
            out_shape=outs,
            scratch_shapes=scratch,
            compiler_params=params_for(28),
            cost_estimate=pl.CostEstimate(flops=4000000000 * pairs, bytes_accessed=8000000, transcendentals=0),
            name="decode",
        )(rows[part], hbm(cross_query), hbm(cross_keyval), fold, head_rows, *extra)
    points, grads = past

    own_grad, square = pl.pallas_call(
        combine_kernel,
        in_specs=[scalar, inside, inside],
        out_shape=(shape((16, 256), F32), shape((groups, 128), F32)),
        compiler_params=params_for(16),
        name="combine",
    )(me.reshape(1), graph.reshape(1, -1), exchange(grads, "dev"))
    total = groups * PEERS * (2 * (TOK + 12) + 13 * PAIRS)
    new_depth, new_cameras, new_params = pl.pallas_call(
        functools.partial(update_kernel, float(total)),
        out_shape=(shape((2, TOK), F32), shape((2, 12), F32), shape((PAIRS, 13), F32)),
        compiler_params=params_for(16),
        name="update",
    )(exchange(square, "grp"), own_grad, depth_map[0], cameras[0], pair_params[0])
    return (
        points.reshape(1, PAIRS, 2, 4, TOK),
        new_depth[None],
        new_cameras[None],
        new_params[None],
    )


def solution(mesh):
    placed = (
        P("grp", "dev", None, None),
        P("grp", "dev"),
        P("grp", "dev", None),
        P("grp", "dev", None),
        P("grp", None, None),
        P("grp", "dev", None),
        P(),
        P(),
        P(),
        P(),
        P(),
    )
    return jax.shard_map(
        on_device,
        mesh=mesh,
        in_specs=placed,
        out_specs=(
            P("grp", "dev", None, None, None),
            P("grp", "dev", None),
            P("grp", "dev", None),
            P("grp", "dev", None),
        ),
        check_vma=False,
    )
```

```python
import functools
import math

import jax
import jax.numpy as jnp
from jax import lax
from jax.experimental import pallas as pl
from jax.experimental.pallas import tpu as pltpu
from jax.sharding import PartitionSpec as P

HEADS = 12
HD = 64
DD = 768
TOK = 192
GW = 16
PEERS = 32
REFS = 8
PAIRS = 4
PIECE = 12
WIDE = 384
GROUPS = 3
LOW = 32

norm_eps = 1e-06
stat_eps = 1e-06
step_rate = 0.3

F32 = jnp.float32
BF16 = jnp.bfloat16
NT = (((1,), (1,)), ((), ()))
MIB = 1024 * 1024


def params_for(mib):
    return pltpu.CompilerParams(vmem_limit_bytes=mib * MIB)


def dot(left, right):
    return jnp.dot(left, right, preferred_element_type=F32)


def dot_nt(left, right):
    return lax.dot_general(left, right, NT, preferred_element_type=F32)


def one_hot(pick):
    return jnp.where(pick, 1.0, 0.0).astype(BF16)


def spread_order(group):
    row = lax.broadcasted_iota(jnp.int32, (64, TOK), 0)
    slot = group * 8 + (row & 7)
    first = (row >> 3) * PIECE + slot
    second = first + jnp.where(slot < 16, 92, 80)
    source = jnp.where(slot < PIECE, first, second)
    return one_hot(source == lax.broadcasted_iota(jnp.int32, (64, TOK), 1))


def gather_order():
    size = 4 * REFS * PIECE
    row = lax.broadcasted_iota(jnp.int32, (size, size), 0)
    image = (row * 1366) >> 16
    rest = row - image * 48
    source = (rest * 43) >> 9
    inner = rest - source * PIECE
    came = source * (REFS * PIECE) + jnp.where(inner < 8, image * 8 + inner, REFS * 8 + image * 4 + inner - 8)
    return one_hot(came == lax.broadcasted_iota(jnp.int32, (size, size), 1))


def embed_kernel(tokens_hbm, weight_hbm, depth_hbm, camera_hbm, focal_hbm, out_hbm,
                 tokens_ref, weight_ref, depth_ref, camera_ref, focal_ref, emb_ref, out_ref, sems):
    copies = [
        pltpu.make_async_copy(tokens_hbm, tokens_ref, sems.at[0]),
        pltpu.make_async_copy(weight_hbm.at[:, pl.ds(0, WIDE)], weight_ref.at[0], sems.at[1]),
        pltpu.make_async_copy(weight_hbm.at[:, pl.ds(WIDE, WIDE)], weight_ref.at[1], sems.at[2]),
        pltpu.make_async_copy(depth_hbm, depth_ref, sems.at[3]),
        pltpu.make_async_copy(camera_hbm, camera_ref, sems.at[4]),
        pltpu.make_async_copy(focal_hbm, focal_ref, sems.at[5]),
    ]
    for copy in copies:
        copy.start()
    orders = [spread_order(group) for group in range(GROUPS)]
    for copy in copies[3:]:
        copy.wait()
    depth = depth_ref[...].astype(F32)
    tail = jnp.concatenate([depth[:, 128:TOK], jnp.zeros((2, 64), F32)], axis=1)
    lane = lax.broadcasted_iota(jnp.int32, (2, 128), 1)
    camera = camera_ref[...].astype(F32)
    focal = focal_ref[...].astype(F32)
    upper = lax.broadcasted_iota(jnp.int32, (2, 128), 0) == 0
    for i in range(12):
        tail = jnp.where(lane == 64 + i, camera[:, i : i + 1], tail)
    tail = jnp.where(lane == 76, jnp.where(upper, focal[:, 0:1], focal[:, 1:2]), tail)
    head = depth[:, 0:128]
    geo = jnp.concatenate([head[0:1], tail[0:1], head[1:2], tail[1:2], jnp.zeros((4, 128), F32)], axis=0)
    geo = jnp.concatenate([geo, geo], axis=0).astype(BF16)
    for two in range(PEERS // 2):
        out_ref[two * 16 : two * 16 + 16, GROUPS * WIDE :] = geo
    copies[0].wait()
    sends = []
    for half in range(2):
        copies[1 + half].wait()
        emb_ref[...] = dot(tokens_ref[...], weight_ref[half]).astype(BF16)
        for part in range(2):
            at = part * 96
            rows = jnp.concatenate([emb_ref[at : at + 96], emb_ref[TOK + at : TOK + at + 96]], axis=0)
            to = pl.ds((2 * half + part) * 64, 64)
            for group in range(GROUPS):
                out_ref[to, group * WIDE : (group + 1) * WIDE] = dot(orders[group], rows).astype(BF16)
            sends.append(pltpu.make_async_copy(out_ref.at[to], out_hbm.at[to], sems.at[6 + 2 * half + part]))
            sends[-1].start()
    for send in sends:
        send.wait()


def select_kernel(rows_ref, long_ref, short_ref, own_ref, after_ref, out_hbm, geo_ref, out_ref, sems):
    total = rows_ref.shape[0]
    outer = jnp.concatenate([rows_ref[:, 0:WIDE], rows_ref[:, 2 * WIDE : 3 * WIDE]], axis=0)
    middle = rows_ref[:, WIDE : 2 * WIDE]
    outer_lane = lax.broadcasted_iota(jnp.int32, (64 * REFS, 2 * total), 1)
    middle_lane = lax.broadcasted_iota(jnp.int32, (32 * REFS, total), 1)
    size = 8 * REFS * PIECE
    copies = []
    for step in range(PEERS // 8):
        long_at = long_ref[step * 64 * REFS : (step + 1) * 64 * REFS]
        short_at = short_ref[step * 32 * REFS : (step + 1) * 32 * REFS]
        long = dot(one_hot(long_at == outer_lane), outer)
        short = dot(one_hot(short_at == middle_lane), middle)
        pieces = []
        for peer in range(8):
            pieces.append(long[peer * 8 * REFS : (peer + 1) * 8 * REFS])
            pieces.append(short[peer * 4 * REFS : (peer + 1) * 4 * REFS])
        at = pl.ds(step * size, size)
        out_ref[at, :] = jnp.concatenate(pieces, axis=0).astype(BF16)
        copies.append(pltpu.make_async_copy(out_ref.at[at], out_hbm.at[at], sems.at[step]))
        copies[-1].start()
    own_lane = lax.broadcasted_iota(jnp.int32, (16, total), 1)
    own = own_ref[...]
    for half in range(2):
        found = dot(one_hot(own + half == own_lane), rows_ref[:, GROUPS * WIDE :])
        geo_ref[:, half * 128 : half * 128 + 128] = found[0:REFS]
    for copy in copies:
        copy.wait()


def fold_kernel(head_ref, out_hbm, value_hbm, fold_ref, out_ref, value_ref, sems):
    copies = []
    for view in range(2):
        copies.append(pltpu.make_async_copy(out_hbm.at[view], out_ref.at[view], sems.at[2 * view]))
        copies.append(
            pltpu.make_async_copy(value_hbm.at[view, :, pl.ds(DD, DD)], value_ref.at[view], sems.at[2 * view + 1])
        )
    for copy in copies:
        copy.start()
    lane = lax.broadcasted_iota(jnp.int32, (16, DD), 1)
    for view in range(2):
        copies[2 * view].wait()
        both = dot_nt(head_ref[view], out_ref[view])
        high = both.astype(BF16).astype(F32)
        low = (both - high).astype(BF16).astype(F32)
        pair = jnp.concatenate([high[0:8], low[0:8]], axis=0)
        left = jnp.concatenate(
            [jnp.where(lane // HD == head, pair, 0.0).astype(BF16) for head in range(HEADS)], axis=0
        )
        copies[2 * view + 1].wait()
        full = dot_nt(left, value_ref[view])
        for head in range(HEADS):
            term = full[head * 16 : head * 16 + 8] + full[head * 16 + 8 : head * 16 + 16]
            top = term.astype(BF16).astype(F32)
            rest = term - top
            fold_ref[view, head * 16 : head * 16 + 16] = jnp.concatenate([top, rest], axis=0).astype(BF16)


def view_gradients(outs, geo, par):
    token = lax.broadcasted_iota(jnp.int32, (REFS, TOK), 1)
    column = (token & (GW - 1)).astype(F32) - (GW - 1) / 2.0
    row_pos = (token >> 4).astype(F32) - (TOK // GW - 1) / 2.0
    depth = geo[:, 0:TOK]
    cam = [geo[:, TOK + i : TOK + i + 1] for i in range(12)]
    focal = geo[:, TOK + 12 : TOK + 13]
    ray = [column / focal, row_pos / focal, jnp.ones_like(column)]
    cam_points = [depth * ray[0], depth * ray[1], depth]
    scale = par[:, 0:1]
    mat = [par[:, 1 + i : 2 + i] for i in range(9)]
    shift = [par[:, 10 + i : 11 + i] for i in range(3)]
    points = outs[:3]
    confidence = outs[3]
    fitted, weighted, ray_image = [], [], []
    for r in range(3):
        world = cam[3 * r] * cam_points[0] + cam[3 * r + 1] * cam_points[1] + cam[3 * r + 2] * cam_points[2]
        world = world + cam[9 + r]
        fit = mat[3 * r] * points[0] + mat[3 * r + 1] * points[1] + mat[3 * r + 2] * points[2] + shift[r]
        fitted.append(fit)
        weighted.append((2.0 * confidence) * (world - scale * fit))
        ray_image.append(cam[3 * r] * ray[0] + cam[3 * r + 1] * ray[1] + cam[3 * r + 2])
    grad_depth = weighted[0] * ray_image[0] + weighted[1] * ray_image[1] + weighted[2] * ray_image[2]

    def total(x):
        return jnp.sum(x, axis=1, keepdims=True)

    sums = [total(w) for w in weighted]
    entries = [total(weighted[r] * cam_points[c]) for r in range(3) for c in range(3)] + sums
    entries.append(-total(weighted[0] * fitted[0] + weighted[1] * fitted[1] + weighted[2] * fitted[2]))
    entries += [-scale * total(weighted[r] * points[c]) for r in range(3) for c in range(3)]
    entries += [-scale * s for s in sums]
    lane = lax.broadcasted_iota(jnp.int32, (REFS, 64), 1)
    tail = jnp.zeros((REFS, 64), F32)
    for i, entry in enumerate(entries):
        high = entry.astype(BF16).astype(F32)
        tail = jnp.where(lane == i, high, jnp.where(lane == LOW + i, entry - high, tail))
    return grad_depth, tail


def decode_kernel(
    rows_ref, query_hbm, key_hbm, fold_ref, head_ref, geo_ref, par_ref,
    points_ref, grad_ref, o_ref, query_ref, key_ref, x_ref, n_ref, q_ref, k_ref, u_ref, e_ref, sems,
):
    copies = []
    for view in range(2):
        copies.append(pltpu.make_async_copy(query_hbm.at[view], query_ref.at[view], sems.at[2 * view]))
        copies.append(
            pltpu.make_async_copy(key_hbm.at[view, :, pl.ds(0, DD)], key_ref.at[view], sems.at[2 * view + 1])
        )
    for copy in copies:
        copy.start()
    order = gather_order()
    size = 4 * REFS * PIECE
    for part in range(PEERS // 4):
        mixed = dot(order, rows_ref[part * size : (part + 1) * size]).astype(BF16)
        cols = slice((part // 4) * WIDE, (part // 4 + 1) * WIDE)
        for image in range(REFS):
            at = (image // 2) * TOK + (part % 4) * 48
            x_ref[image % 2, at : at + 48, cols] = mixed[image * 48 : image * 48 + 48]

    for slot in range(2):
        for pair in range(PAIRS):
            at = pl.ds(pair * TOK, TOK)
            wide = x_ref[slot, at, :].astype(F32)
            centred = wide - jnp.mean(wide, axis=-1, keepdims=True)
            spread = jnp.mean(centred * centred, axis=-1, keepdims=True)
            n_ref[slot, at, :] = (centred * lax.rsqrt(spread + norm_eps)).astype(BF16)

    ones_row = jnp.where(lax.broadcasted_iota(jnp.int32, (8, TOK), 0) == 4, 1.0, 0.0)
    for view in range(2):
        for pair in range(PAIRS):
            at = pl.ds(pair * TOK, TOK)
            value = dot_nt(fold_ref[view], n_ref[1 - view, at, :])
            for head in range(HEADS):
                term = value[head * 16 : head * 16 + 8] + value[head * 16 + 8 : head * 16 + 16] + ones_row
                u_ref[view, pair, head * 16 : head * 16 + 16] = jnp.concatenate(
                    [term, jnp.zeros_like(term)], axis=0
                ).astype(BF16)
            e_ref[view, pair] = dot_nt(head_ref[view], x_ref[view, at, :])[0:8]

    half_of = lax.broadcasted_iota(jnp.int32, (TOK, 2 * HD), 1) // HD
    block_of = lax.broadcasted_iota(jnp.int32, (8, 4 * TOK), 1) // TOK
    factor = math.log2(math.e) / math.sqrt(HD)

    def project(view):
        copies[2 * view].wait()
        q_ref[view] = dot(n_ref[view], query_ref[view]).astype(BF16)
        copies[2 * view + 1].wait()
        k_ref[view] = dot(n_ref[1 - view], key_ref[view]).astype(BF16)

    def scores_of(view, pair, four):
        at = pl.ds(pair * TOK, TOK)
        parts = []
        for two in range(2 * four, 2 * four + 2):
            side = slice(two * 2 * HD, (two + 1) * 2 * HD)
            queries = q_ref[view, at, side]
            blocks = jnp.concatenate(
                [jnp.where(half_of == head, queries, jnp.zeros_like(queries)) for head in range(2)], axis=0
            )
            parts.append(dot_nt(k_ref[view, at, side], blocks))
        return jnp.concatenate(parts, axis=1)

    def probs_of(scores):
        top = jnp.max(scores, axis=0, keepdims=True)
        return jnp.exp2((scores - top) * factor).astype(BF16)

    def context_of(unit, probs):
        view, pair, four = unit
        mixed = dot(u_ref[view, pair, four * 64 : four * 64 + 64], probs)
        own = mixed[0:8]
        for head in range(1, 4):
            own = jnp.where(block_of == head, mixed[head * 16 : head * 16 + 8], own)
        sums[view, pair] = sums.get((view, pair), 0.0) + own * (1.0 / own[4:5])

    units = [(view, pair, four) for view in range(2) for pair in range(PAIRS) for four in range(HEADS // 4)]
    sums = {}
    project(0)
    ahead = [scores_of(*unit) for unit in units[:2]]
    probs = None
    for i, unit in enumerate(units):
        if i == 2:
            project(1)
        scores = ahead.pop(0)
        if i + 2 < len(units):
            ahead.append(scores_of(*units[i + 2]))
        behind = probs
        probs = probs_of(scores)
        if i > 0:
            context_of(units[i - 1], behind)
    context_of(units[-1], probs)
    for (view, pair), acc in sums.items():
        acc = acc[:, 0:TOK] + acc[:, TOK : 2 * TOK] + acc[:, 2 * TOK : 3 * TOK] + acc[:, 3 * TOK :]
        acc = acc + e_ref[view, pair]
        sub = lax.broadcasted_iota(jnp.int32, (8, TOK), 0)
        acc = jnp.where(sub == 3, 1.0 + jnp.exp(acc), acc)
        for c in range(4):
            o_ref[c, 2 * pair + view : 2 * pair + view + 1, :] = acc[c : c + 1]

    outs = [o_ref[c] for c in range(4)]
    for c in range(4):
        for view in range(REFS):
            points_ref[view, c : c + 1] = outs[c][view : view + 1]
    grad_depth, tail = view_gradients(outs, geo_ref[...], par_ref[...])
    both = jnp.concatenate([grad_depth, tail], axis=1)
    twice = jnp.concatenate([both, both], axis=0).astype(BF16)
    for peer in range(0, PEERS, 2):
        grad_ref[peer * REFS : (peer + 2) * REFS] = twice


def combine_kernel(me_ref, graph_ref, grad_ref, own_ref, square_ref):
    refs = PEERS * REFS
    me = me_ref[0]
    graph = graph_ref[...]
    grads = grad_ref[...]

    def summed(pick):
        sums = dot(jnp.where(pick, 1.0, 0.0).astype(BF16), grads)
        lane = lax.broadcasted_iota(jnp.int32, sums.shape, 1)
        return jnp.where(lane < TOK, sums, sums + pltpu.roll(sums, 256 - LOW, 1)), lane

    image = lax.broadcasted_iota(jnp.int32, (2 * PEERS, refs), 0)
    image_sum, image_lane = summed(graph == image)
    pair = lax.broadcasted_iota(jnp.int32, (refs // 2, refs), 0)
    view = lax.broadcasted_iota(jnp.int32, (refs // 2, refs), 1)
    pair_sum, pair_lane = summed((view >> 1) == pair)
    image_sq = jnp.where(image_lane < TOK + 12, image_sum * image_sum, 0.0)
    pair_sq = jnp.where((pair_lane >= TOK + 12) & (pair_lane < TOK + 25), pair_sum * pair_sum, 0.0)
    square_ref[...] = jnp.full(square_ref.shape, jnp.sum(image_sq) + jnp.sum(pair_sq), F32)
    row = lax.broadcasted_iota(jnp.int32, (16, refs), 0)
    ref = lax.broadcasted_iota(jnp.int32, (16, refs), 1)
    own_image = (row < 2) & (graph == 2 * me + row)
    own_pair = (row >= 8) & (row < 8 + PAIRS) & ((ref >> 1) == PAIRS * me + row - 8)
    own_ref[...] = summed(own_image | own_pair)[0]


def update_kernel(count, square_ref, own_ref, depth_ref, camera_ref, par_ref, depth_out, camera_out, par_out):
    total = jnp.sum(square_ref[...], axis=0, keepdims=True)[:, 0:1]
    step = step_rate / jnp.sqrt(total / count + stat_eps)
    depth_out[...] = depth_ref[...].astype(F32) - step * own_ref[0:2, 0:TOK]
    camera_out[...] = camera_ref[...].astype(F32) - step * own_ref[0:2, TOK : TOK + 12]
    par_out[...] = par_ref[...] - step * own_ref[8 : 8 + PAIRS, TOK + 12 : TOK + 25]


def shape(dims, kind):
    return jax.ShapeDtypeStruct(dims, kind)


def hbm(x):
    return pltpu.with_memory_space_constraint(x, pltpu.HBM)


def on_device(
    enc_tokens, focal_len, depth_map, cameras, pair_graph, pair_params,
    embed_weight, cross_query, cross_keyval, cross_out, point_heads,
):
    me = lax.axis_index("dev")
    groups = lax.axis_size("grp")
    inside = pl.BlockSpec(memory_space=pltpu.VMEM)
    outside = pl.BlockSpec(memory_space=pltpu.HBM)
    scalar = pl.BlockSpec(memory_space=pltpu.SMEM)

    def exchange(x, axis):
        return lax.all_to_all(x, axis, split_axis=0, concat_axis=0, tiled=True)

    tokens = enc_tokens[0].reshape(2 * TOK, -1)
    message_dims = (PEERS * 8, GROUPS * WIDE + 128)
    message = pl.pallas_call(
        embed_kernel,
        in_specs=[outside] * 5,
        out_specs=outside,
        out_shape=shape(message_dims, BF16),
        scratch_shapes=[
            pltpu.VMEM(tokens.shape, BF16),
            pltpu.VMEM((2, embed_weight.shape[0], WIDE), BF16),
            pltpu.VMEM((2, TOK), BF16),
            pltpu.VMEM((2, 12), BF16),
            pltpu.VMEM((1, 2), BF16),
            pltpu.VMEM((2 * TOK, WIDE), BF16),
            pltpu.VMEM(message_dims, BF16),
            pltpu.SemaphoreType.DMA((10,)),
        ],
        compiler_params=params_for(24),
        name="embed",
    )(hbm(tokens), hbm(embed_weight), hbm(depth_map[0]), hbm(cameras[0]), hbm(focal_len))
    spread = exchange(message, "dev")

    head_rows = jnp.pad(jnp.swapaxes(point_heads, 1, 2), ((0, 0), (0, 12), (0, 0)))
    fold = pl.pallas_call(
        fold_kernel,
        in_specs=[inside, outside, outside],
        out_specs=inside,
        out_shape=shape((2, HEADS * 16, DD), BF16),
        scratch_shapes=[
            pltpu.VMEM((2, DD, DD), BF16),
            pltpu.VMEM((2, DD, DD), BF16),
            pltpu.SemaphoreType.DMA((4,)),
        ],
        compiler_params=params_for(20),
        cost_estimate=pl.CostEstimate(flops=2000000000, bytes_accessed=6000000, transcendentals=0),
        name="fold",
    )(head_rows, hbm(cross_out), hbm(cross_keyval))

    graph = pair_graph[0].reshape(PEERS * REFS)
    base = (graph // 2) * 8
    long_rows = (base + (graph % 2) * (PEERS * 8))[:, None] + jnp.arange(8, dtype=jnp.int32)
    short_rows = (base + (graph % 2) * 4)[:, None] + jnp.arange(4, dtype=jnp.int32)
    mine = lax.dynamic_slice_in_dim(graph, me * REFS, REFS)
    own = jnp.pad((mine // 2) * 8 + 2 * (mine % 2), (0, 8))[:, None]
    count = PEERS * REFS * PIECE
    outgoing, my_geo = pl.pallas_call(
        select_kernel,
        in_specs=[inside] * 4 + [pl.BlockSpec(memory_space=pl.ANY)],
        out_specs=(outside, inside),
        out_shape=(shape((count, WIDE), BF16), shape((REFS, 256), F32)),
        scratch_shapes=[pltpu.VMEM((count, WIDE), BF16), pltpu.SemaphoreType.DMA((PEERS // 8,))],
        compiler_params=params_for(20),
        name="select",
    )(spread, long_rows.reshape(-1, 1), short_rows.reshape(-1, 1), own, fold)
    rows = exchange(outgoing, "dev")

    weights = pltpu.VMEM((2, DD, DD), BF16)
    tokens_of = pltpu.VMEM((2, PAIRS * TOK, DD), BF16)
    points, grads = pl.pallas_call(
        decode_kernel,
        in_specs=[inside] + [outside] * 2 + [inside] * 4,
        out_specs=(inside, inside),
        out_shape=(shape((REFS, 4, TOK), F32), shape((PEERS * REFS, 256), BF16)),
        scratch_shapes=[
            pltpu.VMEM((4, REFS, TOK), F32),
            weights,
            weights,
            tokens_of,
            tokens_of,
            tokens_of,
            tokens_of,
            pltpu.VMEM((2, PAIRS, HEADS * 16, TOK), BF16),
            pltpu.VMEM((2, PAIRS, 8, TOK), F32),
            pltpu.SemaphoreType.DMA((4,)),
        ],
        compiler_params=params_for(32),
        name="decode",
    )(rows, hbm(cross_query), hbm(cross_keyval), fold, head_rows, my_geo, jnp.repeat(pair_params[0], 2, axis=0))

    own_grad, square = pl.pallas_call(
        combine_kernel,
        in_specs=[scalar, inside, inside],
        out_shape=(shape((16, 256), F32), shape((groups, 128), F32)),
        compiler_params=params_for(16),
        name="combine",
    )(me.reshape(1), graph.reshape(1, -1), exchange(grads, "dev"))
    total = groups * PEERS * (2 * (TOK + 12) + 13 * PAIRS)
    new_depth, new_cameras, new_params = pl.pallas_call(
        functools.partial(update_kernel, float(total)),
        out_shape=(shape((2, TOK), F32), shape((2, 12), F32), shape((PAIRS, 13), F32)),
        compiler_params=params_for(16),
        name="update",
    )(exchange(square, "grp"), own_grad, depth_map[0], cameras[0], pair_params[0])
    return (
        points.reshape(1, PAIRS, 2, 4, TOK),
        new_depth[None],
        new_cameras[None],
        new_params[None],
    )


def solution(mesh):
    placed = (
        P("grp", "dev", None, None),
        P("grp", "dev"),
        P("grp", "dev", None),
        P("grp", "dev", None),
        P("grp", None, None),
        P("grp", "dev", None),
        P(),
        P(),
        P(),
        P(),
        P(),
    )
    return jax.shard_map(
        on_device,
        mesh=mesh,
        in_specs=placed,
        out_specs=(
            P("grp", "dev", None, None, None),
            P("grp", "dev", None),
            P("grp", "dev", None),
            P("grp", "dev", None),
        ),
        check_vma=False,
    )
```

```python
import functools
import math

import jax
import jax.numpy as jnp
from jax import lax
from jax.experimental import pallas as pl
from jax.experimental.pallas import tpu as pltpu
from jax.sharding import PartitionSpec as P

HEADS = 12
HD = 64
DD = 768
TOK = 192
GW = 16
PEERS = 32
REFS = 8
PAIRS = 4
PIECE = 12
WIDE = 384
GROUPS = 3
LOW = 32

norm_eps = 1e-06
stat_eps = 1e-06
step_rate = 0.3

F32 = jnp.float32
BF16 = jnp.bfloat16
NT = (((1,), (1,)), ((), ()))
MIB = 1024 * 1024


def params_for(mib):
    return pltpu.CompilerParams(vmem_limit_bytes=mib * MIB)


def dot(left, right):
    return jnp.dot(left, right, preferred_element_type=F32)


def dot_nt(left, right):
    return lax.dot_general(left, right, NT, preferred_element_type=F32)


def one_hot(pick):
    return jnp.where(pick, 1.0, 0.0).astype(BF16)


def spread_order():
    row = lax.broadcasted_iota(jnp.int32, (64 * GROUPS, TOK), 0)
    slot = (row >> 6) * 8 + (row & 7)
    first = ((row >> 3) & 7) * PIECE + slot
    second = first + jnp.where(slot < 16, 92, 80)
    source = jnp.where(slot < PIECE, first, second)
    return one_hot(source == lax.broadcasted_iota(jnp.int32, (64 * GROUPS, TOK), 1))


def gather_order():
    size = 4 * REFS * PIECE
    row = lax.broadcasted_iota(jnp.int32, (size, size), 0)
    image = (row * 1366) >> 16
    rest = row - image * 48
    source = (rest * 43) >> 9
    inner = rest - source * PIECE
    came = source * (REFS * PIECE) + jnp.where(inner < 8, image * 8 + inner, REFS * 8 + image * 4 + inner - 8)
    return one_hot(came == lax.broadcasted_iota(jnp.int32, (size, size), 1))


def embed_kernel(tokens_hbm, weight_hbm, depth_hbm, camera_hbm, focal_hbm, out_hbm,
                 tokens_ref, weight_ref, depth_ref, camera_ref, focal_ref, emb_ref, out_ref, sems):
    copies = [
        pltpu.make_async_copy(tokens_hbm, tokens_ref, sems.at[0]),
        pltpu.make_async_copy(weight_hbm.at[:, pl.ds(0, WIDE)], weight_ref.at[0], sems.at[1]),
        pltpu.make_async_copy(weight_hbm.at[:, pl.ds(WIDE, WIDE)], weight_ref.at[1], sems.at[2]),
        pltpu.make_async_copy(depth_hbm, depth_ref, sems.at[3]),
        pltpu.make_async_copy(camera_hbm, camera_ref, sems.at[4]),
        pltpu.make_async_copy(focal_hbm, focal_ref, sems.at[5]),
    ]
    for copy in copies:
        copy.start()
    order = spread_order()
    for copy in copies[3:]:
        copy.wait()
    depth = depth_ref[...].astype(F32)
    tail = jnp.concatenate([depth[:, 128:TOK], jnp.zeros((2, 64), F32)], axis=1)
    lane = lax.broadcasted_iota(jnp.int32, (2, 128), 1)
    camera = camera_ref[...].astype(F32)
    focal = focal_ref[...].astype(F32)
    upper = lax.broadcasted_iota(jnp.int32, (2, 128), 0) == 0
    for i in range(12):
        tail = jnp.where(lane == 64 + i, camera[:, i : i + 1], tail)
    tail = jnp.where(lane == 76, jnp.where(upper, focal[:, 0:1], focal[:, 1:2]), tail)
    head = depth[:, 0:128]
    geo = jnp.concatenate([head[0:1], tail[0:1], head[1:2], tail[1:2], jnp.zeros((4, 128), F32)], axis=0)
    geo = jnp.concatenate([geo, geo], axis=0).astype(BF16)
    for two in range(PEERS // 2):
        out_ref[two * 16 : two * 16 + 16, GROUPS * WIDE :] = geo
    copies[0].wait()
    sends = []
    for half in range(2):
        copies[1 + half].wait()
        emb_ref[...] = dot(tokens_ref[...], weight_ref[half]).astype(BF16)
        for part in range(2):
            at = part * 96
            rows = jnp.concatenate([emb_ref[at : at + 96], emb_ref[TOK + at : TOK + at + 96]], axis=0)
            to = pl.ds((2 * half + part) * 64, 64)
            mixed = dot(order, rows).astype(BF16)
            for group in range(GROUPS):
                out_ref[to, group * WIDE : (group + 1) * WIDE] = mixed[group * 64 : group * 64 + 64]
            sends.append(pltpu.make_async_copy(out_ref.at[to], out_hbm.at[to], sems.at[6 + 2 * half + part]))
            sends[-1].start()
    for send in sends:
        send.wait()


def select_kernel(rows_ref, long_ref, short_ref, own_ref, after_ref, out_hbm, geo_ref, out_ref, sems):
    total = rows_ref.shape[0]
    outer = jnp.concatenate([rows_ref[:, 0:WIDE], rows_ref[:, 2 * WIDE : 3 * WIDE]], axis=0)
    middle = rows_ref[:, WIDE : 2 * WIDE]
    outer_lane = lax.broadcasted_iota(jnp.int32, (128 * REFS, 2 * total), 1)
    middle_lane = lax.broadcasted_iota(jnp.int32, (64 * REFS, total), 1)
    size = 16 * REFS * PIECE
    copies = []
    for step in range(PEERS // 16):
        long_at = long_ref[step * 128 * REFS : (step + 1) * 128 * REFS]
        short_at = short_ref[step * 64 * REFS : (step + 1) * 64 * REFS]
        long = dot(one_hot(long_at == outer_lane), outer)
        short = dot(one_hot(short_at == middle_lane), middle)
        pieces = []
        for peer in range(16):
            pieces.append(long[peer * 8 * REFS : (peer + 1) * 8 * REFS])
            pieces.append(short[peer * 4 * REFS : (peer + 1) * 4 * REFS])
        at = pl.ds(step * size, size)
        out_ref[at, :] = jnp.concatenate(pieces, axis=0).astype(BF16)
        copies.append(pltpu.make_async_copy(out_ref.at[at], out_hbm.at[at], sems.at[step]))
        copies[-1].start()
    own_lane = lax.broadcasted_iota(jnp.int32, (16, total), 1)
    own = own_ref[...]
    for half in range(2):
        found = dot(one_hot(own + half == own_lane), rows_ref[:, GROUPS * WIDE :])
        geo_ref[:, half * 128 : half * 128 + 128] = found[0:REFS]
    for copy in copies:
        copy.wait()


def fold_kernel(head_ref, out_hbm, keyval_hbm, query_hbm, fold_ref, query_ref, key_ref, out_ref, value_ref, sems):
    copies = []
    for view in range(2):
        copies.append(pltpu.make_async_copy(out_hbm.at[view], out_ref.at[view], sems.at[2 * view]))
        copies.append(
            pltpu.make_async_copy(keyval_hbm.at[view, :, pl.ds(DD, DD)], value_ref.at[view], sems.at[2 * view + 1])
        )
        copies.append(pltpu.make_async_copy(query_hbm.at[view], query_ref.at[view], sems.at[4 + 2 * view]))
        copies.append(
            pltpu.make_async_copy(keyval_hbm.at[view, :, pl.ds(0, DD)], key_ref.at[view], sems.at[5 + 2 * view])
        )
    for copy in copies:
        copy.start()
    lane = lax.broadcasted_iota(jnp.int32, (16, DD), 1)
    for view in range(2):
        copies[4 * view].wait()
        both = dot_nt(head_ref[view], out_ref[view])
        high = both.astype(BF16).astype(F32)
        low = (both - high).astype(BF16).astype(F32)
        pair = jnp.concatenate([high[0:8], low[0:8]], axis=0)
        left = jnp.concatenate(
            [jnp.where(lane // HD == head, pair, 0.0).astype(BF16) for head in range(HEADS)], axis=0
        )
        copies[4 * view + 1].wait()
        full = dot_nt(left, value_ref[view])
        for head in range(HEADS):
            term = full[head * 16 : head * 16 + 8] + full[head * 16 + 8 : head * 16 + 16]
            top = term.astype(BF16).astype(F32)
            rest = term - top
            fold_ref[view, head * 16 : head * 16 + 16] = jnp.concatenate([top, rest], axis=0).astype(BF16)
    for view in range(2):
        copies[4 * view + 2].wait()
        copies[4 * view + 3].wait()


def view_gradients(outs, geo, par):
    token = lax.broadcasted_iota(jnp.int32, (REFS, TOK), 1)
    column = (token & (GW - 1)).astype(F32) - (GW - 1) / 2.0
    row_pos = (token >> 4).astype(F32) - (TOK // GW - 1) / 2.0
    depth = geo[:, 0:TOK]
    cam = [geo[:, TOK + i : TOK + i + 1] for i in range(12)]
    focal = geo[:, TOK + 12 : TOK + 13]
    ray = [column / focal, row_pos / focal, jnp.ones_like(column)]
    cam_points = [depth * ray[0], depth * ray[1], depth]
    scale = par[:, 0:1]
    mat = [par[:, 1 + i : 2 + i] for i in range(9)]
    shift = [par[:, 10 + i : 11 + i] for i in range(3)]
    points = outs[:3]
    confidence = outs[3]
    fitted, weighted, ray_image = [], [], []
    for r in range(3):
        world = cam[3 * r] * cam_points[0] + cam[3 * r + 1] * cam_points[1] + cam[3 * r + 2] * cam_points[2]
        world = world + cam[9 + r]
        fit = mat[3 * r] * points[0] + mat[3 * r + 1] * points[1] + mat[3 * r + 2] * points[2] + shift[r]
        fitted.append(fit)
        weighted.append((2.0 * confidence) * (world - scale * fit))
        ray_image.append(cam[3 * r] * ray[0] + cam[3 * r + 1] * ray[1] + cam[3 * r + 2])
    grad_depth = weighted[0] * ray_image[0] + weighted[1] * ray_image[1] + weighted[2] * ray_image[2]

    def total(x):
        return jnp.sum(x, axis=1, keepdims=True)

    sums = [total(w) for w in weighted]
    entries = [total(weighted[r] * cam_points[c]) for r in range(3) for c in range(3)] + sums
    entries.append(-total(weighted[0] * fitted[0] + weighted[1] * fitted[1] + weighted[2] * fitted[2]))
    entries += [-scale * total(weighted[r] * points[c]) for r in range(3) for c in range(3)]
    entries += [-scale * s for s in sums]
    lane = lax.broadcasted_iota(jnp.int32, (REFS, 64), 1)
    tail = jnp.zeros((REFS, 64), F32)
    for i, entry in enumerate(entries):
        high = entry.astype(BF16).astype(F32)
        tail = jnp.where(lane == i, high, jnp.where(lane == LOW + i, entry - high, tail))
    return grad_depth, tail


def decode_kernel(
    rows_ref, query_ref, key_ref, fold_ref, head_ref, geo_ref, par_ref,
    points_ref, grad_ref, o_ref, x_ref, n_ref, q_ref, k_ref, u_ref, e_ref,
):
    order = gather_order()
    size = 4 * REFS * PIECE
    for part in range(PEERS // 4):
        mixed = dot(order, rows_ref[part * size : (part + 1) * size]).astype(BF16)
        cols = slice((part // 4) * WIDE, (part // 4 + 1) * WIDE)
        for image in range(REFS):
            at = (image // 2) * TOK + (part % 4) * 48
            x_ref[image % 2, at : at + 48, cols] = mixed[image * 48 : image * 48 + 48]

    for slot in range(2):
        for pair in range(PAIRS):
            at = pl.ds(pair * TOK, TOK)
            wide = x_ref[slot, at, :].astype(F32)
            centred = wide - jnp.mean(wide, axis=-1, keepdims=True)
            spread = jnp.mean(centred * centred, axis=-1, keepdims=True)
            n_ref[slot, at, :] = (centred * lax.rsqrt(spread + norm_eps)).astype(BF16)

    ones_row = jnp.where(lax.broadcasted_iota(jnp.int32, (8, TOK), 0) == 4, 1.0, 0.0)
    for view in range(2):
        for pair in range(PAIRS):
            at = pl.ds(pair * TOK, TOK)
            value = dot_nt(fold_ref[view], n_ref[1 - view, at, :])
            for head in range(HEADS):
                term = value[head * 16 : head * 16 + 8] + value[head * 16 + 8 : head * 16 + 16] + ones_row
                u_ref[view, pair, head * 16 : head * 16 + 16] = jnp.concatenate(
                    [term, jnp.zeros_like(term)], axis=0
                ).astype(BF16)
            e_ref[view, pair] = dot_nt(head_ref[view], x_ref[view, at, :])[0:8]

    half_of = lax.broadcasted_iota(jnp.int32, (TOK, 2 * HD), 1) // HD
    block_of = lax.broadcasted_iota(jnp.int32, (8, 4 * TOK), 1) // TOK
    factor = math.log2(math.e) / math.sqrt(HD)

    def project(view):
        q_ref[view] = dot(n_ref[view], query_ref[view]).astype(BF16)
        k_ref[view] = dot(n_ref[1 - view], key_ref[view]).astype(BF16)

    def scores_of(view, pair, four):
        at = pl.ds(pair * TOK, TOK)
        parts = []
        for two in range(2 * four, 2 * four + 2):
            side = slice(two * 2 * HD, (two + 1) * 2 * HD)
            queries = q_ref[view, at, side]
            blocks = jnp.concatenate(
                [jnp.where(half_of == head, queries, jnp.zeros_like(queries)) for head in range(2)], axis=0
            )
            parts.append(dot_nt(k_ref[view, at, side], blocks))
        return jnp.concatenate(parts, axis=1)

    def probs_of(scores):
        top = jnp.max(scores, axis=0, keepdims=True)
        return jnp.exp2((scores - top) * factor).astype(BF16)

    def context_of(unit, probs):
        view, pair, four = unit
        mixed = dot(u_ref[view, pair, four * 64 : four * 64 + 64], probs)
        own = mixed[0:8]
        for head in range(1, 4):
            own = jnp.where(block_of == head, mixed[head * 16 : head * 16 + 8], own)
        sums[view, pair] = sums.get((view, pair), 0.0) + own * (1.0 / own[4:5])

    units = [(view, pair, four) for view in range(2) for pair in range(PAIRS) for four in range(HEADS // 4)]
    sums = {}
    project(0)
    ahead = [scores_of(*unit) for unit in units[:2]]
    probs = None
    for i, unit in enumerate(units):
        if i == 2:
            project(1)
        scores = ahead.pop(0)
        if i + 2 < len(units):
            ahead.append(scores_of(*units[i + 2]))
        behind = probs
        probs = probs_of(scores)
        if i > 0:
            context_of(units[i - 1], behind)
    context_of(units[-1], probs)
    for (view, pair), acc in sums.items():
        acc = acc[:, 0:TOK] + acc[:, TOK : 2 * TOK] + acc[:, 2 * TOK : 3 * TOK] + acc[:, 3 * TOK :]
        acc = acc + e_ref[view, pair]
        sub = lax.broadcasted_iota(jnp.int32, (8, TOK), 0)
        acc = jnp.where(sub == 3, 1.0 + jnp.exp(acc), acc)
        for c in range(4):
            o_ref[c, 2 * pair + view : 2 * pair + view + 1, :] = acc[c : c + 1]

    outs = [o_ref[c] for c in range(4)]
    for c in range(4):
        for view in range(REFS):
            points_ref[view, c : c + 1] = outs[c][view : view + 1]
    grad_depth, tail = view_gradients(outs, geo_ref[...], par_ref[...])
    both = jnp.concatenate([grad_depth, tail], axis=1)
    twice = jnp.concatenate([both, both], axis=0).astype(BF16)
    for peer in range(0, PEERS, 2):
        grad_ref[peer * REFS : (peer + 2) * REFS] = twice


def combine_kernel(me_ref, graph_ref, grad_ref, own_ref, square_ref):
    refs = PEERS * REFS
    me = me_ref[0]
    graph = graph_ref[...]
    grads = grad_ref[...]

    def summed(pick):
        sums = dot(jnp.where(pick, 1.0, 0.0).astype(BF16), grads)
        lane = lax.broadcasted_iota(jnp.int32, sums.shape, 1)
        return jnp.where(lane < TOK, sums, sums + pltpu.roll(sums, 256 - LOW, 1)), lane

    image = lax.broadcasted_iota(jnp.int32, (2 * PEERS, refs), 0)
    image_sum, image_lane = summed(graph == image)
    pair = lax.broadcasted_iota(jnp.int32, (refs // 2, refs), 0)
    view = lax.broadcasted_iota(jnp.int32, (refs // 2, refs), 1)
    pair_sum, pair_lane = summed((view >> 1) == pair)
    image_sq = jnp.where(image_lane < TOK + 12, image_sum * image_sum, 0.0)
    pair_sq = jnp.where((pair_lane >= TOK + 12) & (pair_lane < TOK + 25), pair_sum * pair_sum, 0.0)
    square_ref[...] = jnp.full(square_ref.shape, jnp.sum(image_sq) + jnp.sum(pair_sq), F32)
    row = lax.broadcasted_iota(jnp.int32, (16, refs), 0)
    ref = lax.broadcasted_iota(jnp.int32, (16, refs), 1)
    own_image = (row < 2) & (graph == 2 * me + row)
    own_pair = (row >= 8) & (row < 8 + PAIRS) & ((ref >> 1) == PAIRS * me + row - 8)
    own_ref[...] = summed(own_image | own_pair)[0]


def update_kernel(count, square_ref, own_ref, depth_ref, camera_ref, par_ref, depth_out, camera_out, par_out):
    total = jnp.sum(square_ref[...], axis=0, keepdims=True)[:, 0:1]
    step = step_rate / jnp.sqrt(total / count + stat_eps)
    depth_out[...] = depth_ref[...].astype(F32) - step * own_ref[0:2, 0:TOK]
    camera_out[...] = camera_ref[...].astype(F32) - step * own_ref[0:2, TOK : TOK + 12]
    par_out[...] = par_ref[...] - step * own_ref[8 : 8 + PAIRS, TOK + 12 : TOK + 25]


def shape(dims, kind):
    return jax.ShapeDtypeStruct(dims, kind)


def hbm(x):
    return pltpu.with_memory_space_constraint(x, pltpu.HBM)


def on_device(
    enc_tokens, focal_len, depth_map, cameras, pair_graph, pair_params,
    embed_weight, cross_query, cross_keyval, cross_out, point_heads,
):
    me = lax.axis_index("dev")
    groups = lax.axis_size("grp")
    inside = pl.BlockSpec(memory_space=pltpu.VMEM)
    outside = pl.BlockSpec(memory_space=pltpu.HBM)
    scalar = pl.BlockSpec(memory_space=pltpu.SMEM)

    def exchange(x, axis):
        return lax.all_to_all(x, axis, split_axis=0, concat_axis=0, tiled=True)

    tokens = enc_tokens[0].reshape(2 * TOK, -1)
    message_dims = (PEERS * 8, GROUPS * WIDE + 128)
    message = pl.pallas_call(
        embed_kernel,
        in_specs=[outside] * 5,
        out_specs=outside,
        out_shape=shape(message_dims, BF16),
        scratch_shapes=[
            pltpu.VMEM(tokens.shape, BF16),
            pltpu.VMEM((2, embed_weight.shape[0], WIDE), BF16),
            pltpu.VMEM((2, TOK), BF16),
            pltpu.VMEM((2, 12), BF16),
            pltpu.VMEM((1, 2), BF16),
            pltpu.VMEM((2 * TOK, WIDE), BF16),
            pltpu.VMEM(message_dims, BF16),
            pltpu.SemaphoreType.DMA((10,)),
        ],
        compiler_params=params_for(24),
        name="embed",
    )(hbm(tokens), hbm(embed_weight), hbm(depth_map[0]), hbm(cameras[0]), hbm(focal_len))
    spread = exchange(message, "dev")

    head_rows = jnp.pad(jnp.swapaxes(point_heads, 1, 2), ((0, 0), (0, 12), (0, 0)))
    square = shape((2, DD, DD), BF16)
    fold, query, key = pl.pallas_call(
        fold_kernel,
        in_specs=[inside, outside, outside, outside],
        out_specs=(inside, inside, inside),
        out_shape=(shape((2, HEADS * 16, DD), BF16), square, square),
        scratch_shapes=[
            pltpu.VMEM((2, DD, DD), BF16),
            pltpu.VMEM((2, DD, DD), BF16),
            pltpu.SemaphoreType.DMA((8,)),
        ],
        compiler_params=params_for(20),
        cost_estimate=pl.CostEstimate(flops=2000000000, bytes_accessed=6000000, transcendentals=0),
        name="fold",
    )(head_rows, hbm(cross_out), hbm(cross_keyval), hbm(cross_query))

    graph = pair_graph[0].reshape(PEERS * REFS)
    base = (graph // 2) * 8
    long_rows = (base + (graph % 2) * (PEERS * 8))[:, None] + jnp.arange(8, dtype=jnp.int32)
    short_rows = (base + (graph % 2) * 4)[:, None] + jnp.arange(4, dtype=jnp.int32)
    mine = lax.dynamic_slice_in_dim(graph, me * REFS, REFS)
    own = jnp.pad((mine // 2) * 8 + 2 * (mine % 2), (0, 8))[:, None]
    count = PEERS * REFS * PIECE
    outgoing, my_geo = pl.pallas_call(
        select_kernel,
        in_specs=[inside] * 4 + [pl.BlockSpec(memory_space=pl.ANY)],
        out_specs=(outside, inside),
        out_shape=(shape((count, WIDE), BF16), shape((REFS, 256), F32)),
        scratch_shapes=[pltpu.VMEM((count, WIDE), BF16), pltpu.SemaphoreType.DMA((PEERS // 16,))],
        compiler_params=params_for(20),
        name="select",
    )(spread, long_rows.reshape(-1, 1), short_rows.reshape(-1, 1), own, fold)
    rows = exchange(outgoing, "dev")

    tokens_of = pltpu.VMEM((2, PAIRS * TOK, DD), BF16)
    points, grads = pl.pallas_call(
        decode_kernel,
        in_specs=[inside] * 7,
        out_specs=(inside, inside),
        out_shape=(shape((REFS, 4, TOK), F32), shape((PEERS * REFS, 256), BF16)),
        scratch_shapes=[
            pltpu.VMEM((4, REFS, TOK), F32),
            tokens_of,
            tokens_of,
            tokens_of,
            tokens_of,
            pltpu.VMEM((2, PAIRS, HEADS * 16, TOK), BF16),
            pltpu.VMEM((2, PAIRS, 8, TOK), F32),
        ],
        compiler_params=params_for(28),
        name="decode",
    )(rows, query, key, fold, head_rows, my_geo, jnp.repeat(pair_params[0], 2, axis=0))

    own_grad, square = pl.pallas_call(
        combine_kernel,
        in_specs=[scalar, inside, inside],
        out_shape=(shape((16, 256), F32), shape((groups, 128), F32)),
        compiler_params=params_for(16),
        name="combine",
    )(me.reshape(1), graph.reshape(1, -1), exchange(grads, "dev"))
    total = groups * PEERS * (2 * (TOK + 12) + 13 * PAIRS)
    new_depth, new_cameras, new_params = pl.pallas_call(
        functools.partial(update_kernel, float(total)),
        out_shape=(shape((2, TOK), F32), shape((2, 12), F32), shape((PAIRS, 13), F32)),
        compiler_params=params_for(16),
        name="update",
    )(exchange(square, "grp"), own_grad, depth_map[0], cameras[0], pair_params[0])
    return (
        points.reshape(1, PAIRS, 2, 4, TOK),
        new_depth[None],
        new_cameras[None],
        new_params[None],
    )


def solution(mesh):
    placed = (
        P("grp", "dev", None, None),
        P("grp", "dev"),
        P("grp", "dev", None),
        P("grp", "dev", None),
        P("grp", None, None),
        P("grp", "dev", None),
        P(),
        P(),
        P(),
        P(),
        P(),
    )
    return jax.shard_map(
        on_device,
        mesh=mesh,
        in_specs=placed,
        out_specs=(
            P("grp", "dev", None, None, None),
            P("grp", "dev", None),
            P("grp", "dev", None),
            P("grp", "dev", None),
        ),
        check_vma=False,
    )
```

```python
import functools
import math

import jax
import jax.numpy as jnp
import numpy as np
from jax import lax
from jax.experimental import pallas as pl
from jax.experimental.pallas import tpu as pltpu
from jax.sharding import Mesh
from jax.sharding import PartitionSpec as P

HEADS = 12
HD = 64
DD = 768
TOK = 192
GW = 16
PEERS = 32
REFS = 8
PAIRS = 4
PIECE = 12
WIDE = 384
GROUPS = 3
LOW = 32

PLANE = ("x", "c", "y")
HOME = [(rank * 8 + z, z * PEERS + rank) for rank in range(PEERS) for z in range(8)]

norm_eps = 1e-06
stat_eps = 1e-06
step_rate = 0.3

F32 = jnp.float32
BF16 = jnp.bfloat16
NT = (((1,), (1,)), ((), ()))
MIB = 1024 * 1024


def params_for(mib):
    return pltpu.CompilerParams(vmem_limit_bytes=mib * MIB)


def dot(left, right):
    return jnp.dot(left, right, preferred_element_type=F32)


def dot_nt(left, right):
    return lax.dot_general(left, right, NT, preferred_element_type=F32)


def one_hot(pick):
    return jnp.where(pick, 1.0, 0.0).astype(BF16)


def spread_order():
    row = lax.broadcasted_iota(jnp.int32, (64 * GROUPS, TOK), 0)
    slot = (row >> 6) * 8 + (row & 7)
    first = ((row >> 3) & 7) * PIECE + slot
    second = first + jnp.where(slot < 16, 92, 80)
    source = jnp.where(slot < PIECE, first, second)
    return one_hot(source == lax.broadcasted_iota(jnp.int32, (64 * GROUPS, TOK), 1))


def gather_order():
    size = 4 * REFS * PIECE
    row = lax.broadcasted_iota(jnp.int32, (size, size), 0)
    image = (row * 1366) >> 16
    rest = row - image * 48
    source = (rest * 43) >> 9
    inner = rest - source * PIECE
    came = source * (REFS * PIECE) + jnp.where(inner < 8, image * 8 + inner, REFS * 8 + image * 4 + inner - 8)
    return one_hot(came == lax.broadcasted_iota(jnp.int32, (size, size), 1))


def embed_kernel(tokens_hbm, weight_hbm, depth_hbm, camera_hbm, focal_hbm, graph_hbm, par_hbm, out_hbm,
                 tokens_ref, weight_ref, depth_ref, camera_ref, focal_ref, graph_ref, par_ref, emb_ref, out_ref, sems):
    copies = [
        pltpu.make_async_copy(tokens_hbm, tokens_ref, sems.at[0]),
        pltpu.make_async_copy(weight_hbm.at[:, pl.ds(0, WIDE)], weight_ref.at[0], sems.at[1]),
        pltpu.make_async_copy(weight_hbm.at[:, pl.ds(WIDE, WIDE)], weight_ref.at[1], sems.at[2]),
        pltpu.make_async_copy(depth_hbm, depth_ref, sems.at[3]),
        pltpu.make_async_copy(camera_hbm, camera_ref, sems.at[4]),
        pltpu.make_async_copy(focal_hbm, focal_ref, sems.at[5]),
        pltpu.make_async_copy(graph_hbm, graph_ref, sems.at[10]),
        pltpu.make_async_copy(par_hbm, par_ref, sems.at[11]),
    ]
    for copy in copies:
        copy.start()
    order = spread_order()
    for copy in copies[3:]:
        copy.wait()
    depth = depth_ref[...].astype(F32)
    tail = jnp.concatenate([depth[:, 128:TOK], jnp.zeros((2, 64), F32)], axis=1)
    lane = lax.broadcasted_iota(jnp.int32, (2, 128), 1)
    camera = camera_ref[...].astype(F32)
    focal = focal_ref[...].astype(F32)
    upper = lax.broadcasted_iota(jnp.int32, (2, 128), 0) == 0
    for i in range(12):
        tail = jnp.where(lane == 64 + i, camera[:, i : i + 1], tail)
    tail = jnp.where(lane == 76, jnp.where(upper, focal[:, 0:1], focal[:, 1:2]), tail)
    head = depth[:, 0:128]
    par = jnp.concatenate([par_ref[...], jnp.zeros((PAIRS, 3), F32)], axis=1)
    par = jnp.concatenate([par[pair : pair + 1] for pair in range(PAIRS)], axis=1)
    high = par.astype(BF16).astype(F32)
    middle = (par - high).astype(BF16).astype(F32)
    last = jnp.concatenate([par - high - middle, jnp.zeros((1, 64), F32)], axis=1)
    par = jnp.concatenate([high, middle], axis=1)
    pairs = graph_ref[...].astype(F32)
    geo = jnp.concatenate([head[0:1], tail[0:1], head[1:2], tail[1:2], pairs, par, last], axis=0)
    geo = jnp.concatenate([geo, geo], axis=0).astype(BF16)
    for two in range(PEERS // 2):
        out_ref[two * 16 : two * 16 + 16, GROUPS * WIDE :] = geo
    copies[0].wait()
    sends = []
    for half in range(2):
        copies[1 + half].wait()
        emb_ref[...] = dot(tokens_ref[...], weight_ref[half]).astype(BF16)
        for part in range(2):
            at = part * 96
            rows = jnp.concatenate([emb_ref[at : at + 96], emb_ref[TOK + at : TOK + at + 96]], axis=0)
            to = pl.ds((2 * half + part) * 64, 64)
            mixed = dot(order, rows).astype(BF16)
            for group in range(GROUPS):
                out_ref[to, group * WIDE : (group + 1) * WIDE] = mixed[group * 64 : group * 64 + 64]
            sends.append(pltpu.make_async_copy(out_ref.at[to], out_hbm.at[to], sems.at[6 + 2 * half + part]))
            sends[-1].start()
    for send in sends:
        send.wait()


def index_kernel(rank_ref, tile_ref, long_ref, short_ref, own_ref, graph_ref):
    rank = rank_ref[0]
    total = PEERS * 8
    ids = tile_ref[...].astype(F32)[4:6].astype(jnp.int32)
    owner = ids >> 1
    place = (owner & 7) * 4 + (owner >> 3)
    odd = ids & 1
    table = jnp.concatenate([place * 8 + odd * total, place * 8 + odd * 4, place * 8 + odd * 2, ids], axis=0)
    table = jnp.concatenate([table, table], axis=0).astype(F32).astype(BF16)

    def looked_up(first, count, per_pair, shift, column):
        row = lax.broadcasted_iota(jnp.int32, (count, 128), 0) + first
        lane = lax.broadcasted_iota(jnp.int32, (count, 128), 1)
        found = dot_nt(one_hot((row >> per_pair) == lane), table)
        slot = (lax.broadcasted_iota(jnp.int32, (count, 1), 0) >> shift) & 1
        return jnp.where(slot == 1, found[:, column + 1 : column + 2], found[:, column : column + 1]).astype(jnp.int32)

    long_row = lax.broadcasted_iota(jnp.int32, (8 * total, 1), 0) & 7
    short_row = lax.broadcasted_iota(jnp.int32, (4 * total, 1), 0) & 3
    long_ref[...] = looked_up(0, 8 * total, 4, 3, 0) + long_row
    short_ref[...] = looked_up(0, 4 * total, 3, 2, 2) + short_row
    own_ref[...] = looked_up(rank * REFS, 16, 1, 0, 4)
    lane = lax.broadcasted_iota(jnp.int32, (128, 256), 1)
    pair = lax.broadcasted_iota(jnp.int32, (128, 256), 0)
    spread = [dot(table, one_hot(lane == 2 * pair + slot))[6 + slot : 7 + slot] for slot in range(2)]
    graph_ref[...] = (spread[0] + spread[1]).astype(jnp.int32)


def select_kernel(rank_ref, rows_ref, long_ref, short_ref, own_ref, after_ref, out_hbm, geo_ref, par_ref, out_ref, sems):
    rank = rank_ref[0]
    total = rows_ref.shape[0]
    tile = rows_ref[:, GROUPS * WIDE :]
    outer = jnp.concatenate([rows_ref[:, 0:WIDE], rows_ref[:, 2 * WIDE : 3 * WIDE]], axis=0)
    middle = rows_ref[:, WIDE : 2 * WIDE]
    outer_lane = lax.broadcasted_iota(jnp.int32, (128 * REFS, 2 * total), 1)
    middle_lane = lax.broadcasted_iota(jnp.int32, (64 * REFS, total), 1)
    size = 16 * REFS * PIECE
    copies = []
    for step in range(PEERS // 16):
        long_at = long_ref[step * 128 * REFS : (step + 1) * 128 * REFS]
        short_at = short_ref[step * 64 * REFS : (step + 1) * 64 * REFS]
        long = dot(one_hot(long_at == outer_lane), outer)
        short = dot(one_hot(short_at == middle_lane), middle)
        pieces = []
        for peer in range(16):
            pieces.append(long[peer * 8 * REFS : (peer + 1) * 8 * REFS])
            pieces.append(short[peer * 4 * REFS : (peer + 1) * 4 * REFS])
        at = pl.ds(step * size, size)
        out_ref[at, :] = jnp.concatenate(pieces, axis=0).astype(BF16)
        copies.append(pltpu.make_async_copy(out_ref.at[at], out_hbm.at[at], sems.at[step]))
        copies[-1].start()
    own_lane = lax.broadcasted_iota(jnp.int32, (16, total), 1)
    own = own_ref[...]
    for half in range(2):
        found = dot(one_hot(own + half == own_lane), tile)
        geo_ref[:, half * 128 : half * 128 + 128] = found[0:REFS]
    mine = ((rank & 7) * 4 + (rank >> 3)) * 8 + 6
    row = lax.broadcasted_iota(jnp.int32, (16, total), 0)
    par = dot(one_hot((row < 2) & (own_lane == mine + row)), tile)
    par = par[0:1] + pltpu.roll(par[0:1], 64, 1) + par[1:2]
    views = []
    for pair in range(PAIRS):
        views += [par if pair == 0 else pltpu.roll(par, 128 - 16 * pair, 1)] * 2
    par_ref[...] = jnp.concatenate(views, axis=0)
    for copy in copies:
        copy.wait()


def fold_kernel(head_ref, out_hbm, keyval_hbm, query_hbm, fold_ref, query_ref, key_ref, out_ref, value_ref, sems):
    copies = []
    for view in range(2):
        copies.append(pltpu.make_async_copy(out_hbm.at[view], out_ref.at[view], sems.at[2 * view]))
        copies.append(
            pltpu.make_async_copy(keyval_hbm.at[view, :, pl.ds(DD, DD)], value_ref.at[view], sems.at[2 * view + 1])
        )
        copies.append(pltpu.make_async_copy(query_hbm.at[view], query_ref.at[view], sems.at[4 + 2 * view]))
        copies.append(
            pltpu.make_async_copy(keyval_hbm.at[view, :, pl.ds(0, DD)], key_ref.at[view], sems.at[5 + 2 * view])
        )
    for copy in copies:
        copy.start()
    lane = lax.broadcasted_iota(jnp.int32, (16, DD), 1)
    for view in range(2):
        copies[4 * view].wait()
        both = dot_nt(head_ref[view], out_ref[view])
        high = both.astype(BF16).astype(F32)
        low = (both - high).astype(BF16).astype(F32)
        pair = jnp.concatenate([high[0:8], low[0:8]], axis=0)
        left = jnp.concatenate(
            [jnp.where(lane // HD == head, pair, 0.0).astype(BF16) for head in range(HEADS)], axis=0
        )
        copies[4 * view + 1].wait()
        full = dot_nt(left, value_ref[view])
        for head in range(HEADS):
            term = full[head * 16 : head * 16 + 8] + full[head * 16 + 8 : head * 16 + 16]
            top = term.astype(BF16).astype(F32)
            rest = term - top
            fold_ref[view, head * 16 : head * 16 + 16] = jnp.concatenate([top, rest], axis=0).astype(BF16)
    for view in range(2):
        copies[4 * view + 2].wait()
        copies[4 * view + 3].wait()


def view_gradients(outs, geo, par):
    token = lax.broadcasted_iota(jnp.int32, (REFS, TOK), 1)
    column = (token & (GW - 1)).astype(F32) - (GW - 1) / 2.0
    row_pos = (token >> 4).astype(F32) - (TOK // GW - 1) / 2.0
    depth = geo[:, 0:TOK]
    cam = [geo[:, TOK + i : TOK + i + 1] for i in range(12)]
    focal = geo[:, TOK + 12 : TOK + 13]
    ray = [column / focal, row_pos / focal, jnp.ones_like(column)]
    cam_points = [depth * ray[0], depth * ray[1], depth]
    scale = par[:, 0:1]
    mat = [par[:, 1 + i : 2 + i] for i in range(9)]
    shift = [par[:, 10 + i : 11 + i] for i in range(3)]
    points = outs[:3]
    confidence = outs[3]
    fitted, weighted, ray_image = [], [], []
    for r in range(3):
        world = cam[3 * r] * cam_points[0] + cam[3 * r + 1] * cam_points[1] + cam[3 * r + 2] * cam_points[2]
        world = world + cam[9 + r]
        fit = mat[3 * r] * points[0] + mat[3 * r + 1] * points[1] + mat[3 * r + 2] * points[2] + shift[r]
        fitted.append(fit)
        weighted.append((2.0 * confidence) * (world - scale * fit))
        ray_image.append(cam[3 * r] * ray[0] + cam[3 * r + 1] * ray[1] + cam[3 * r + 2])
    grad_depth = weighted[0] * ray_image[0] + weighted[1] * ray_image[1] + weighted[2] * ray_image[2]

    def total(x):
        return jnp.sum(x, axis=1, keepdims=True)

    sums = [total(w) for w in weighted]
    entries = [total(weighted[r] * cam_points[c]) for r in range(3) for c in range(3)] + sums
    entries.append(-total(weighted[0] * fitted[0] + weighted[1] * fitted[1] + weighted[2] * fitted[2]))
    entries += [-scale * total(weighted[r] * points[c]) for r in range(3) for c in range(3)]
    entries += [-scale * s for s in sums]
    lane = lax.broadcasted_iota(jnp.int32, (REFS, 64), 1)
    tail = jnp.zeros((REFS, 64), F32)
    for i, entry in enumerate(entries):
        high = entry.astype(BF16).astype(F32)
        tail = jnp.where(lane == i, high, jnp.where(lane == LOW + i, entry - high, tail))
    return grad_depth, tail


def decode_kernel(
    rows_ref, query_ref, key_ref, fold_ref, head_ref, geo_ref, par_ref,
    points_ref, grad_ref, o_ref, x_ref, n_ref, q_ref, k_ref, u_ref, e_ref,
):
    order = gather_order()
    size = 4 * REFS * PIECE
    for part in range(PEERS // 4):
        mixed = dot(order, rows_ref[part * size : (part + 1) * size]).astype(BF16)
        cols = slice((part // 4) * WIDE, (part // 4 + 1) * WIDE)
        for image in range(REFS):
            at = (image // 2) * TOK + (part % 4) * 48
            x_ref[image % 2, at : at + 48, cols] = mixed[image * 48 : image * 48 + 48]

    for slot in range(2):
        for pair in range(PAIRS):
            at = pl.ds(pair * TOK, TOK)
            wide = x_ref[slot, at, :].astype(F32)
            centred = wide - jnp.mean(wide, axis=-1, keepdims=True)
            spread = jnp.mean(centred * centred, axis=-1, keepdims=True)
            n_ref[slot, at, :] = (centred * lax.rsqrt(spread + norm_eps)).astype(BF16)

    ones_row = jnp.where(lax.broadcasted_iota(jnp.int32, (8, TOK), 0) == 4, 1.0, 0.0)
    for view in range(2):
        for pair in range(PAIRS):
            at = pl.ds(pair * TOK, TOK)
            value = dot_nt(fold_ref[view], n_ref[1 - view, at, :])
            for head in range(HEADS):
                term = value[head * 16 : head * 16 + 8] + value[head * 16 + 8 : head * 16 + 16] + ones_row
                u_ref[view, pair, head * 16 : head * 16 + 16] = jnp.concatenate(
                    [term, jnp.zeros_like(term)], axis=0
                ).astype(BF16)
            e_ref[view, pair] = dot_nt(head_ref[view], x_ref[view, at, :])[0:8]

    half_of = lax.broadcasted_iota(jnp.int32, (TOK, 2 * HD), 1) // HD
    block_of = lax.broadcasted_iota(jnp.int32, (8, 4 * TOK), 1) // TOK
    factor = math.log2(math.e) / math.sqrt(HD)

    def project(view):
        q_ref[view] = dot(n_ref[view], query_ref[view]).astype(BF16)
        k_ref[view] = dot(n_ref[1 - view], key_ref[view]).astype(BF16)

    def scores_of(view, pair, four):
        at = pl.ds(pair * TOK, TOK)
        parts = []
        for two in range(2 * four, 2 * four + 2):
            side = slice(two * 2 * HD, (two + 1) * 2 * HD)
            queries = q_ref[view, at, side]
            blocks = jnp.concatenate(
                [jnp.where(half_of == head, queries, jnp.zeros_like(queries)) for head in range(2)], axis=0
            )
            parts.append(dot_nt(k_ref[view, at, side], blocks))
        return jnp.concatenate(parts, axis=1)

    def probs_of(scores):
        top = jnp.max(scores, axis=0, keepdims=True)
        return jnp.exp2((scores - top) * factor).astype(BF16)

    def context_of(unit, probs):
        view, pair, four = unit
        mixed = dot(u_ref[view, pair, four * 64 : four * 64 + 64], probs)
        own = mixed[0:8]
        for head in range(1, 4):
            own = jnp.where(block_of == head, mixed[head * 16 : head * 16 + 8], own)
        sums[view, pair] = sums.get((view, pair), 0.0) + own * (1.0 / own[4:5])

    units = [(view, pair, four) for view in range(2) for pair in range(PAIRS) for four in range(HEADS // 4)]
    sums = {}
    project(0)
    ahead = [scores_of(*unit) for unit in units[:2]]
    probs = None
    for i, unit in enumerate(units):
        if i == 2:
            project(1)
        scores = ahead.pop(0)
        if i + 2 < len(units):
            ahead.append(scores_of(*units[i + 2]))
        behind = probs
        probs = probs_of(scores)
        if i > 0:
            context_of(units[i - 1], behind)
    context_of(units[-1], probs)
    for (view, pair), acc in sums.items():
        acc = acc[:, 0:TOK] + acc[:, TOK : 2 * TOK] + acc[:, 2 * TOK : 3 * TOK] + acc[:, 3 * TOK :]
        acc = acc + e_ref[view, pair]
        sub = lax.broadcasted_iota(jnp.int32, (8, TOK), 0)
        acc = jnp.where(sub == 3, 1.0 + jnp.exp(acc), acc)
        for c in range(4):
            o_ref[c, 2 * pair + view : 2 * pair + view + 1, :] = acc[c : c + 1]

    outs = [o_ref[c] for c in range(4)]
    for c in range(4):
        for view in range(REFS):
            points_ref[view, c : c + 1] = outs[c][view : view + 1]
    grad_depth, tail = view_gradients(outs, geo_ref[...], par_ref[...])
    both = jnp.concatenate([grad_depth, tail], axis=1)
    twice = jnp.concatenate([both, both], axis=0).astype(BF16)
    for peer in range(0, PEERS, 2):
        grad_ref[peer * REFS : (peer + 2) * REFS] = twice


def combine_kernel(me_ref, graph_ref, grad_ref, own_ref, square_ref):
    refs = PEERS * REFS
    me = me_ref[0]
    graph = graph_ref[...]
    grads = grad_ref[...]

    def summed(pick):
        sums = dot(jnp.where(pick, 1.0, 0.0).astype(BF16), grads)
        lane = lax.broadcasted_iota(jnp.int32, sums.shape, 1)
        return jnp.where(lane < TOK, sums, sums + pltpu.roll(sums, 256 - LOW, 1)), lane

    image = lax.broadcasted_iota(jnp.int32, (2 * PEERS, refs), 0)
    image_sum, image_lane = summed(graph == image)
    pair = lax.broadcasted_iota(jnp.int32, (refs // 2, refs), 0)
    view = lax.broadcasted_iota(jnp.int32, (refs // 2, refs), 1)
    pair_sum, pair_lane = summed((view >> 1) == pair)
    image_sq = jnp.where(image_lane < TOK + 12, image_sum * image_sum, 0.0)
    pair_sq = jnp.where((pair_lane >= TOK + 12) & (pair_lane < TOK + 25), pair_sum * pair_sum, 0.0)
    square_ref[...] = jnp.full(square_ref.shape, jnp.sum(image_sq) + jnp.sum(pair_sq), F32)
    row = lax.broadcasted_iota(jnp.int32, (16, refs), 0)
    ref = lax.broadcasted_iota(jnp.int32, (16, refs), 1)
    own_image = (row < 2) & (graph == 2 * me + row)
    own_pair = (row >= 8) & (row < 8 + PAIRS) & ((ref >> 1) == PAIRS * me + row - 8)
    own_ref[...] = summed(own_image | own_pair)[0]


def update_kernel(
    count, square_ref, own_ref, depth_ref, camera_ref, par_ref, points_ref, depth_out, camera_out, par_out, points_out
):
    points_out[...] = points_ref[...]
    total = jnp.sum(square_ref[...], axis=0, keepdims=True)[:, 0:1]
    step = step_rate / jnp.sqrt(total / count + stat_eps)
    depth_out[...] = depth_ref[...].astype(F32) - step * own_ref[0:2, 0:TOK]
    camera_out[...] = camera_ref[...].astype(F32) - step * own_ref[0:2, TOK : TOK + 12]
    par_out[...] = par_ref[...] - step * own_ref[8 : 8 + PAIRS, TOK + 12 : TOK + 25]


def shape(dims, kind):
    return jax.ShapeDtypeStruct(dims, kind)


def hbm(x):
    return pltpu.with_memory_space_constraint(x, pltpu.HBM)


def on_device(
    enc_tokens, focal_len, depth_map, cameras, pair_graph, pair_params,
    embed_weight, cross_query, cross_keyval, cross_out, point_heads,
):
    rank = lax.axis_index(PLANE)
    groups = lax.axis_size("z")
    inside = pl.BlockSpec(memory_space=pltpu.VMEM)
    outside = pl.BlockSpec(memory_space=pltpu.HBM)
    scalar = pl.BlockSpec(memory_space=pltpu.SMEM)

    def exchange(x, axis):
        return lax.all_to_all(x, axis, split_axis=0, concat_axis=0, tiled=True)

    tokens = enc_tokens[0].reshape(2 * TOK, -1)
    message_dims = (PEERS * 8, GROUPS * WIDE + 128)
    message = pl.pallas_call(
        embed_kernel,
        in_specs=[outside] * 7,
        out_specs=outside,
        out_shape=shape(message_dims, BF16),
        scratch_shapes=[
            pltpu.VMEM(tokens.shape, BF16),
            pltpu.VMEM((2, embed_weight.shape[0], WIDE), BF16),
            pltpu.VMEM((2, TOK), BF16),
            pltpu.VMEM((2, 12), BF16),
            pltpu.VMEM((1, 2), BF16),
            pltpu.VMEM((2, 128), jnp.int32),
            pltpu.VMEM((PAIRS, 13), F32),
            pltpu.VMEM((2 * TOK, WIDE), BF16),
            pltpu.VMEM(message_dims, BF16),
            pltpu.SemaphoreType.DMA((12,)),
        ],
        compiler_params=params_for(24),
        name="embed",
    )(hbm(tokens), hbm(embed_weight), hbm(depth_map[0]), hbm(cameras[0]), hbm(focal_len),
      hbm(jnp.swapaxes(pair_graph[0], 0, 1)), hbm(pair_params[0]))
    across = exchange(message, ("x", "c"))
    tile = lax.dynamic_slice(across, (lax.axis_index("z") * PEERS, GROUPS * WIDE), (8, 128))
    spread = exchange(across, ("z", "y"))
    long_rows, short_rows, own, graph = pl.pallas_call(
        index_kernel,
        in_specs=[scalar, inside],
        out_specs=(inside,) * 4,
        out_shape=(
            shape((PEERS * REFS * 8, 1), jnp.int32),
            shape((PEERS * REFS * 4, 1), jnp.int32),
            shape((16, 1), jnp.int32),
            shape((1, PEERS * REFS), jnp.int32),
        ),
        compiler_params=params_for(20),
        cost_estimate=pl.CostEstimate(flops=500000000, bytes_accessed=2000000, transcendentals=0),
        name="index",
    )(rank.reshape(1), tile)

    head_rows = jnp.pad(jnp.swapaxes(point_heads, 1, 2), ((0, 0), (0, 12), (0, 0)))
    square = shape((2, DD, DD), BF16)
    fold, query, key = pl.pallas_call(
        fold_kernel,
        in_specs=[inside, outside, outside, outside],
        out_specs=(inside, inside, inside),
        out_shape=(shape((2, HEADS * 16, DD), BF16), square, square),
        scratch_shapes=[
            pltpu.VMEM((2, DD, DD), BF16),
            pltpu.VMEM((2, DD, DD), BF16),
            pltpu.SemaphoreType.DMA((8,)),
        ],
        compiler_params=params_for(20),
        cost_estimate=pl.CostEstimate(flops=2000000000, bytes_accessed=6000000, transcendentals=0),
        name="fold",
    )(head_rows, hbm(cross_out), hbm(cross_keyval), hbm(cross_query))

    count = PEERS * REFS * PIECE
    outgoing, my_geo, view_par = pl.pallas_call(
        select_kernel,
        in_specs=[scalar] + [inside] * 4 + [pl.BlockSpec(memory_space=pl.ANY)],
        out_specs=(outside, inside, inside),
        out_shape=(
            shape((count, WIDE), BF16),
            shape((REFS, 256), F32),
            shape((REFS, 128), F32),
        ),
        scratch_shapes=[pltpu.VMEM((count, WIDE), BF16), pltpu.SemaphoreType.DMA((PEERS // 16,))],
        compiler_params=params_for(28),
        name="select",
    )(rank.reshape(1), spread, long_rows, short_rows, own, fold)
    rows = exchange(outgoing, PLANE)

    tokens_of = pltpu.VMEM((2, PAIRS * TOK, DD), BF16)
    points, grads = pl.pallas_call(
        decode_kernel,
        in_specs=[inside] * 7,
        out_specs=(inside, inside),
        out_shape=(shape((REFS, 4, TOK), F32), shape((PEERS * REFS, 256), BF16)),
        scratch_shapes=[
            pltpu.VMEM((4, REFS, TOK), F32),
            tokens_of,
            tokens_of,
            tokens_of,
            tokens_of,
            pltpu.VMEM((2, PAIRS, HEADS * 16, TOK), BF16),
            pltpu.VMEM((2, PAIRS, 8, TOK), F32),
        ],
        compiler_params=params_for(28),
        name="decode",
    )(rows, query, key, fold, head_rows, my_geo, view_par)

    own_grad, square = pl.pallas_call(
        combine_kernel,
        in_specs=[scalar, inside, inside],
        out_shape=(shape((16, 256), F32), shape((groups, 128), F32)),
        compiler_params=params_for(16),
        name="combine",
    )(rank.reshape(1), graph, exchange(grads, PLANE))
    own_grad = lax.ppermute(own_grad, PLANE + ("z",), HOME)
    points = lax.ppermute(points, PLANE + ("z",), HOME)
    total = groups * PEERS * (2 * (TOK + 12) + 13 * PAIRS)
    new_depth, new_cameras, new_params, points = pl.pallas_call(
        functools.partial(update_kernel, float(total)),
        out_shape=(shape((2, TOK), F32), shape((2, 12), F32), shape((PAIRS, 13), F32), shape(points.shape, F32)),
        compiler_params=params_for(16),
        name="update",
    )(exchange(square, "z"), own_grad, depth_map[0], cameras[0], pair_params[0], points)
    return (
        points.reshape(1, PAIRS, 2, 4, TOK),
        new_depth[None],
        new_cameras[None],
        new_params[None],
    )


def solution(mesh):
    axes = ("x", "c", "y", "z")
    split = Mesh(np.asarray(mesh.devices).reshape(4, 2, 4, 8), axes)
    grp, dev = ("x", "c"), ("y", "z")
    placed = (
        P(grp, dev, None, None),
        P(grp, dev),
        P(grp, dev, None),
        P(grp, dev, None),
        P(grp, None, None),
        P(grp, dev, None),
        P(),
        P(),
        P(),
        P(),
        P(),
    )
    return jax.shard_map(
        on_device,
        mesh=split,
        in_specs=placed,
        out_specs=(
            P(grp, dev, None, None, None),
            P(grp, dev, None),
            P(grp, dev, None),
            P(grp, dev, None),
        ),
        check_vma=False,
    )
```

```python
import functools
import math

import jax
import jax.numpy as jnp
import numpy as np
from jax import lax
from jax.experimental import pallas as pl
from jax.experimental.pallas import tpu as pltpu
from jax.sharding import Mesh
from jax.sharding import PartitionSpec as P

HEADS = 12
HD = 64
DD = 768
TOK = 192
GW = 16
PEERS = 32
REFS = 8
PAIRS = 4
PIECE = 12
WIDE = 384
GROUPS = 3
LOW = 32

PLANE = ("x", "c", "y")
HOME = [(rank * 8 + z, z * PEERS + rank) for rank in range(PEERS) for z in range(8)]

norm_eps = 1e-06
stat_eps = 1e-06
step_rate = 0.3

F32 = jnp.float32
BF16 = jnp.bfloat16
NT = (((1,), (1,)), ((), ()))
MIB = 1024 * 1024


def params_for(mib):
    return pltpu.CompilerParams(vmem_limit_bytes=mib * MIB)


def dot(left, right):
    return jnp.dot(left, right, preferred_element_type=F32)


def dot_nt(left, right):
    return lax.dot_general(left, right, NT, preferred_element_type=F32)


def one_hot(pick):
    return jnp.where(pick, 1.0, 0.0).astype(BF16)


def spread_order():
    row = lax.broadcasted_iota(jnp.int32, (64 * GROUPS, TOK), 0)
    slot = (row >> 6) * 8 + (row & 7)
    first = ((row >> 3) & 7) * PIECE + slot
    second = first + jnp.where(slot < 16, 92, 80)
    source = jnp.where(slot < PIECE, first, second)
    return one_hot(source == lax.broadcasted_iota(jnp.int32, (64 * GROUPS, TOK), 1))


def gather_order():
    size = 4 * REFS * PIECE
    row = lax.broadcasted_iota(jnp.int32, (size, size), 0)
    image = (row * 1366) >> 16
    rest = row - image * 48
    source = (rest * 43) >> 9
    inner = rest - source * PIECE
    came = source * (REFS * PIECE) + jnp.where(inner < 8, image * 8 + inner, REFS * 8 + image * 4 + inner - 8)
    return one_hot(came == lax.broadcasted_iota(jnp.int32, (size, size), 1))


def embed_kernel(tokens_hbm, weight_hbm, depth_hbm, camera_hbm, focal_hbm, graph_hbm, par_hbm, out_hbm,
                 tokens_ref, weight_ref, depth_ref, camera_ref, focal_ref, graph_ref, par_ref, emb_ref, out_ref, sems):
    copies = [
        pltpu.make_async_copy(tokens_hbm, tokens_ref, sems.at[0]),
        pltpu.make_async_copy(weight_hbm.at[:, pl.ds(0, WIDE)], weight_ref.at[0], sems.at[1]),
        pltpu.make_async_copy(weight_hbm.at[:, pl.ds(WIDE, WIDE)], weight_ref.at[1], sems.at[2]),
        pltpu.make_async_copy(depth_hbm, depth_ref, sems.at[3]),
        pltpu.make_async_copy(camera_hbm, camera_ref, sems.at[4]),
        pltpu.make_async_copy(focal_hbm, focal_ref, sems.at[5]),
        pltpu.make_async_copy(graph_hbm, graph_ref, sems.at[10]),
        pltpu.make_async_copy(par_hbm, par_ref, sems.at[11]),
    ]
    for copy in copies[3:] + copies[:3]:
        copy.start()
    order = spread_order()
    for copy in copies[3:]:
        copy.wait()
    depth = depth_ref[...].astype(F32)
    tail = jnp.concatenate([depth[:, 128:TOK], jnp.zeros((2, 64), F32)], axis=1)
    lane = lax.broadcasted_iota(jnp.int32, (2, 128), 1)
    camera = camera_ref[...].astype(F32)
    focal = focal_ref[...].astype(F32)
    upper = lax.broadcasted_iota(jnp.int32, (2, 128), 0) == 0
    for i in range(12):
        tail = jnp.where(lane == 64 + i, camera[:, i : i + 1], tail)
    tail = jnp.where(lane == 76, jnp.where(upper, focal[:, 0:1], focal[:, 1:2]), tail)
    head = depth[:, 0:128]
    par = jnp.concatenate([par_ref[...], jnp.zeros((PAIRS, 3), F32)], axis=1)
    par = jnp.concatenate([par[pair : pair + 1] for pair in range(PAIRS)], axis=1)
    high = par.astype(BF16).astype(F32)
    middle = (par - high).astype(BF16).astype(F32)
    last = jnp.concatenate([par - high - middle, jnp.zeros((1, 64), F32)], axis=1)
    par = jnp.concatenate([high, middle], axis=1)
    pairs = graph_ref[...].astype(F32)
    geo = jnp.concatenate([head[0:1], tail[0:1], head[1:2], tail[1:2], pairs, par, last], axis=0)
    geo = jnp.concatenate([geo, geo], axis=0).astype(BF16)
    for two in range(PEERS // 2):
        out_ref[two * 16 : two * 16 + 16, GROUPS * WIDE :] = geo
    copies[0].wait()
    sends = []
    for half in range(2):
        copies[1 + half].wait()
        emb_ref[...] = dot(tokens_ref[...], weight_ref[half]).astype(BF16)
        for part in range(2):
            at = part * 96
            rows = jnp.concatenate([emb_ref[at : at + 96], emb_ref[TOK + at : TOK + at + 96]], axis=0)
            to = pl.ds((2 * half + part) * 64, 64)
            mixed = dot(order, rows).astype(BF16)
            for group in range(GROUPS):
                out_ref[to, group * WIDE : (group + 1) * WIDE] = mixed[group * 64 : group * 64 + 64]
            sends.append(pltpu.make_async_copy(out_ref.at[to], out_hbm.at[to], sems.at[6 + 2 * half + part]))
            sends[-1].start()
    for send in sends:
        send.wait()


def index_kernel(rank_ref, tile_ref, long_ref, short_ref, own_ref, graph_ref):
    rank = rank_ref[0]
    total = PEERS * 8
    ids = tile_ref[...].astype(F32)[4:6].astype(jnp.int32)
    owner = ids >> 1
    place = (owner & 7) * 4 + (owner >> 3)
    odd = ids & 1
    table = jnp.concatenate([place * 8 + odd * total, place * 8 + odd * 4, place * 8 + odd * 2, ids], axis=0)
    table = jnp.concatenate([table, table], axis=0).astype(F32).astype(BF16)

    def looked_up(first, count, per_pair, shift, column):
        row = lax.broadcasted_iota(jnp.int32, (count, 128), 0) + first
        lane = lax.broadcasted_iota(jnp.int32, (count, 128), 1)
        found = dot_nt(one_hot((row >> per_pair) == lane), table)
        slot = (lax.broadcasted_iota(jnp.int32, (count, 1), 0) >> shift) & 1
        return jnp.where(slot == 1, found[:, column + 1 : column + 2], found[:, column : column + 1]).astype(jnp.int32)

    long_row = lax.broadcasted_iota(jnp.int32, (8 * total, 1), 0) & 7
    short_row = lax.broadcasted_iota(jnp.int32, (4 * total, 1), 0) & 3
    long_ref[...] = looked_up(0, 8 * total, 4, 3, 0) + long_row
    short_ref[...] = looked_up(0, 4 * total, 3, 2, 2) + short_row
    own_ref[...] = looked_up(rank * REFS, 16, 1, 0, 4)
    lane = lax.broadcasted_iota(jnp.int32, (128, 256), 1)
    pair = lax.broadcasted_iota(jnp.int32, (128, 256), 0)
    spread = [dot(table, one_hot(lane == 2 * pair + slot))[6 + slot : 7 + slot] for slot in range(2)]
    graph_ref[...] = (spread[0] + spread[1]).astype(jnp.int32)


def select_kernel(rank_ref, rows_ref, long_ref, short_ref, own_ref, after_ref, out_hbm, geo_ref, par_ref, out_ref, sems):
    rank = rank_ref[0]
    total = rows_ref.shape[0]
    tile = rows_ref[:, GROUPS * WIDE :]
    outer = jnp.concatenate([rows_ref[:, 0:WIDE], rows_ref[:, 2 * WIDE : 3 * WIDE]], axis=0)
    middle = rows_ref[:, WIDE : 2 * WIDE]
    outer_lane = lax.broadcasted_iota(jnp.int32, (256 * REFS, 2 * total), 1)
    middle_lane = lax.broadcasted_iota(jnp.int32, (128 * REFS, total), 1)
    size = 32 * REFS * PIECE
    copies = []
    for step in range(PEERS // 32):
        long_at = long_ref[step * 256 * REFS : (step + 1) * 256 * REFS]
        short_at = short_ref[step * 128 * REFS : (step + 1) * 128 * REFS]
        long = dot(one_hot(long_at == outer_lane), outer)
        short = dot(one_hot(short_at == middle_lane), middle)
        pieces = []
        for peer in range(32):
            pieces.append(long[peer * 8 * REFS : (peer + 1) * 8 * REFS])
            pieces.append(short[peer * 4 * REFS : (peer + 1) * 4 * REFS])
        at = pl.ds(step * size, size)
        out_ref[at, :] = jnp.concatenate(pieces, axis=0).astype(BF16)
        copies.append(pltpu.make_async_copy(out_ref.at[at], out_hbm.at[at], sems.at[step]))
        copies[-1].start()
    own_lane = lax.broadcasted_iota(jnp.int32, (16, total), 1)
    own = own_ref[...]
    for half in range(2):
        found = dot(one_hot(own + half == own_lane), tile)
        geo_ref[:, half * 128 : half * 128 + 128] = found[0:REFS]
    mine = ((rank & 7) * 4 + (rank >> 3)) * 8 + 6
    row = lax.broadcasted_iota(jnp.int32, (16, total), 0)
    par = dot(one_hot((row < 2) & (own_lane == mine + row)), tile)
    par = par[0:1] + pltpu.roll(par[0:1], 64, 1) + par[1:2]
    views = []
    for pair in range(PAIRS):
        views += [par if pair == 0 else pltpu.roll(par, 128 - 16 * pair, 1)] * 2
    par_ref[...] = jnp.concatenate(views, axis=0)
    for copy in copies:
        copy.wait()


def fold_kernel(head_ref, out_hbm, keyval_hbm, query_hbm, fold_ref, query_ref, key_ref, out_ref, value_ref, sems):
    copies = []
    for view in range(2):
        copies.append(pltpu.make_async_copy(out_hbm.at[view], out_ref.at[view], sems.at[2 * view]))
        copies.append(
            pltpu.make_async_copy(keyval_hbm.at[view, :, pl.ds(DD, DD)], value_ref.at[view], sems.at[2 * view + 1])
        )
        copies.append(pltpu.make_async_copy(query_hbm.at[view], query_ref.at[view], sems.at[4 + 2 * view]))
        copies.append(
            pltpu.make_async_copy(keyval_hbm.at[view, :, pl.ds(0, DD)], key_ref.at[view], sems.at[5 + 2 * view])
        )
    for copy in copies:
        copy.start()
    lane = lax.broadcasted_iota(jnp.int32, (16, DD), 1)
    for view in range(2):
        copies[4 * view].wait()
        both = dot_nt(head_ref[view], out_ref[view])
        high = both.astype(BF16).astype(F32)
        low = (both - high).astype(BF16).astype(F32)
        pair = jnp.concatenate([high[0:8], low[0:8]], axis=0)
        left = jnp.concatenate(
            [jnp.where(lane // HD == head, pair, 0.0).astype(BF16) for head in range(HEADS)], axis=0
        )
        copies[4 * view + 1].wait()
        full = dot_nt(left, value_ref[view])
        for head in range(HEADS):
            term = full[head * 16 : head * 16 + 8] + full[head * 16 + 8 : head * 16 + 16]
            top = term.astype(BF16).astype(F32)
            rest = term - top
            fold_ref[view, head * 16 : head * 16 + 16] = jnp.concatenate([top, rest], axis=0).astype(BF16)
    for view in range(2):
        copies[4 * view + 2].wait()
        copies[4 * view + 3].wait()


def view_gradients(outs, geo, par):
    token = lax.broadcasted_iota(jnp.int32, (REFS, TOK), 1)
    column = (token & (GW - 1)).astype(F32) - (GW - 1) / 2.0
    row_pos = (token >> 4).astype(F32) - (TOK // GW - 1) / 2.0
    depth = geo[:, 0:TOK]
    cam = [geo[:, TOK + i : TOK + i + 1] for i in range(12)]
    focal = geo[:, TOK + 12 : TOK + 13]
    ray = [column / focal, row_pos / focal, jnp.ones_like(column)]
    cam_points = [depth * ray[0], depth * ray[1], depth]
    scale = par[:, 0:1]
    mat = [par[:, 1 + i : 2 + i] for i in range(9)]
    shift = [par[:, 10 + i : 11 + i] for i in range(3)]
    points = outs[:3]
    confidence = outs[3]
    fitted, weighted, ray_image = [], [], []
    for r in range(3):
        world = cam[3 * r] * cam_points[0] + cam[3 * r + 1] * cam_points[1] + cam[3 * r + 2] * cam_points[2]
        world = world + cam[9 + r]
        fit = mat[3 * r] * points[0] + mat[3 * r + 1] * points[1] + mat[3 * r + 2] * points[2] + shift[r]
        fitted.append(fit)
        weighted.append((2.0 * confidence) * (world - scale * fit))
        ray_image.append(cam[3 * r] * ray[0] + cam[3 * r + 1] * ray[1] + cam[3 * r + 2])
    grad_depth = weighted[0] * ray_image[0] + weighted[1] * ray_image[1] + weighted[2] * ray_image[2]

    def total(x):
        return jnp.sum(x, axis=1, keepdims=True)

    sums = [total(w) for w in weighted]
    entries = [total(weighted[r] * cam_points[c]) for r in range(3) for c in range(3)] + sums
    entries.append(-total(weighted[0] * fitted[0] + weighted[1] * fitted[1] + weighted[2] * fitted[2]))
    entries += [-scale * total(weighted[r] * points[c]) for r in range(3) for c in range(3)]
    entries += [-scale * s for s in sums]
    lane = lax.broadcasted_iota(jnp.int32, (REFS, 64), 1)
    tail = jnp.zeros((REFS, 64), F32)
    for i, entry in enumerate(entries):
        high = entry.astype(BF16).astype(F32)
        tail = jnp.where(lane == i, high, jnp.where(lane == LOW + i, entry - high, tail))
    return grad_depth, tail


def decode_kernel(
    rows_ref, query_ref, key_ref, fold_ref, head_ref, geo_ref, par_ref,
    points_ref, grad_ref, o_ref, x_ref, n_ref, q_ref, k_ref, u_ref, e_ref,
):
    order = gather_order()
    size = 4 * REFS * PIECE
    for part in range(PEERS // 8):
        sides = [rows_ref[(part + 4 * side) * size : (part + 4 * side + 1) * size] for side in range(2)]
        mixed = dot(order, jnp.concatenate(sides, axis=1)).astype(BF16)
        for image in range(REFS):
            at = (image // 2) * TOK + part * 48
            x_ref[image % 2, at : at + 48] = mixed[image * 48 : image * 48 + 48]

    for slot in range(2):
        for pair in range(PAIRS):
            at = pl.ds(pair * TOK, TOK)
            wide = x_ref[slot, at, :].astype(F32)
            centred = wide - jnp.mean(wide, axis=-1, keepdims=True)
            spread = jnp.mean(centred * centred, axis=-1, keepdims=True)
            n_ref[slot, at, :] = (centred * lax.rsqrt(spread + norm_eps)).astype(BF16)

    ones_row = jnp.where(lax.broadcasted_iota(jnp.int32, (8, TOK), 0) == 4, 1.0, 0.0)
    for view in range(2):
        for pair in range(PAIRS):
            at = pl.ds(pair * TOK, TOK)
            value = dot_nt(fold_ref[view], n_ref[1 - view, at, :])
            for head in range(HEADS):
                term = value[head * 16 : head * 16 + 8] + value[head * 16 + 8 : head * 16 + 16] + ones_row
                u_ref[view, pair, head * 16 : head * 16 + 16] = jnp.concatenate(
                    [term, jnp.zeros_like(term)], axis=0
                ).astype(BF16)
            e_ref[view, pair] = dot_nt(head_ref[view], x_ref[view, at, :])[0:8]

    half_of = lax.broadcasted_iota(jnp.int32, (TOK, 2 * HD), 1) // HD
    block_of = lax.broadcasted_iota(jnp.int32, (8, 4 * TOK), 1) // TOK
    factor = math.log2(math.e) / math.sqrt(HD)

    def project(view):
        q_ref[view] = dot(n_ref[view], query_ref[view]).astype(BF16)
        k_ref[view] = dot(n_ref[1 - view], key_ref[view]).astype(BF16)

    def scores_of(view, pair, four):
        at = pl.ds(pair * TOK, TOK)
        parts = []
        for two in range(2 * four, 2 * four + 2):
            side = slice(two * 2 * HD, (two + 1) * 2 * HD)
            queries = q_ref[view, at, side]
            blocks = jnp.concatenate(
                [jnp.where(half_of == head, queries, jnp.zeros_like(queries)) for head in range(2)], axis=0
            )
            parts.append(dot_nt(k_ref[view, at, side], blocks))
        return jnp.concatenate(parts, axis=1)

    def probs_of(scores):
        top = jnp.max(scores, axis=0, keepdims=True)
        return jnp.exp2((scores - top) * factor).astype(BF16)

    def context_of(unit, probs):
        view, pair, four = unit
        mixed = dot(u_ref[view, pair, four * 64 : four * 64 + 64], probs)
        own = mixed[0:8]
        for head in range(1, 4):
            own = jnp.where(block_of == head, mixed[head * 16 : head * 16 + 8], own)
        sums[view, pair] = sums.get((view, pair), 0.0) + own * (1.0 / own[4:5])

    units = [(view, pair, four) for view in range(2) for pair in range(PAIRS) for four in range(HEADS // 4)]
    sums = {}
    project(0)
    ahead = [scores_of(*unit) for unit in units[:2]]
    probs = None
    for i, unit in enumerate(units):
        if i == 2:
            project(1)
        scores = ahead.pop(0)
        if i + 2 < len(units):
            ahead.append(scores_of(*units[i + 2]))
        behind = probs
        probs = probs_of(scores)
        if i > 0:
            context_of(units[i - 1], behind)
    context_of(units[-1], probs)
    for (view, pair), acc in sums.items():
        acc = acc[:, 0:TOK] + acc[:, TOK : 2 * TOK] + acc[:, 2 * TOK : 3 * TOK] + acc[:, 3 * TOK :]
        acc = acc + e_ref[view, pair]
        sub = lax.broadcasted_iota(jnp.int32, (8, TOK), 0)
        acc = jnp.where(sub == 3, 1.0 + jnp.exp(acc), acc)
        for c in range(4):
            o_ref[c, 2 * pair + view : 2 * pair + view + 1, :] = acc[c : c + 1]

    outs = [o_ref[c] for c in range(4)]
    for c in range(4):
        for view in range(REFS):
            points_ref[view, c : c + 1] = outs[c][view : view + 1]
    grad_depth, tail = view_gradients(outs, geo_ref[...], par_ref[...])
    both = jnp.concatenate([grad_depth, tail], axis=1)
    twice = jnp.concatenate([both, both], axis=0).astype(BF16)
    for peer in range(0, PEERS, 2):
        grad_ref[peer * REFS : (peer + 2) * REFS] = twice


def combine_kernel(me_ref, graph_ref, grad_ref, own_ref, square_ref):
    refs = PEERS * REFS
    me = me_ref[0]
    graph = graph_ref[...]
    grads = grad_ref[...]

    def summed(pick):
        sums = dot(jnp.where(pick, 1.0, 0.0).astype(BF16), grads)
        lane = lax.broadcasted_iota(jnp.int32, sums.shape, 1)
        return jnp.where(lane < TOK, sums, sums + pltpu.roll(sums, 256 - LOW, 1)), lane

    image = lax.broadcasted_iota(jnp.int32, (2 * PEERS, refs), 0)
    image_sum, image_lane = summed(graph == image)
    pair = lax.broadcasted_iota(jnp.int32, (refs // 2, refs), 0)
    view = lax.broadcasted_iota(jnp.int32, (refs // 2, refs), 1)
    pair_sum, pair_lane = summed((view >> 1) == pair)
    image_sq = jnp.where(image_lane < TOK + 12, image_sum * image_sum, 0.0)
    pair_sq = jnp.where((pair_lane >= TOK + 12) & (pair_lane < TOK + 25), pair_sum * pair_sum, 0.0)
    square_ref[...] = jnp.full(square_ref.shape, jnp.sum(image_sq) + jnp.sum(pair_sq), F32)
    row = lax.broadcasted_iota(jnp.int32, (16, refs), 0)
    ref = lax.broadcasted_iota(jnp.int32, (16, refs), 1)
    own_image = (row < 2) & (graph == 2 * me + row)
    own_pair = (row >= 8) & (row < 8 + PAIRS) & ((ref >> 1) == PAIRS * me + row - 8)
    own_ref[...] = summed(own_image | own_pair)[0]


def update_kernel(
    count, square_ref, own_ref, depth_ref, camera_ref, par_ref, points_ref, depth_out, camera_out, par_out, points_out
):
    points_out[...] = points_ref[...]
    total = jnp.sum(square_ref[...], axis=0, keepdims=True)[:, 0:1]
    step = step_rate / jnp.sqrt(total / count + stat_eps)
    depth_out[...] = depth_ref[...].astype(F32) - step * own_ref[0:2, 0:TOK]
    camera_out[...] = camera_ref[...].astype(F32) - step * own_ref[0:2, TOK : TOK + 12]
    par_out[...] = par_ref[...] - step * own_ref[8 : 8 + PAIRS, TOK + 12 : TOK + 25]


def shape(dims, kind):
    return jax.ShapeDtypeStruct(dims, kind)


def hbm(x):
    return pltpu.with_memory_space_constraint(x, pltpu.HBM)


def on_device(
    enc_tokens, focal_len, depth_map, cameras, pair_graph, pair_params,
    embed_weight, cross_query, cross_keyval, cross_out, point_heads,
):
    rank = lax.axis_index(PLANE)
    groups = lax.axis_size("z")
    inside = pl.BlockSpec(memory_space=pltpu.VMEM)
    outside = pl.BlockSpec(memory_space=pltpu.HBM)
    scalar = pl.BlockSpec(memory_space=pltpu.SMEM)

    def exchange(x, axis):
        return lax.all_to_all(x, axis, split_axis=0, concat_axis=0, tiled=True)

    tokens = enc_tokens[0].reshape(2 * TOK, -1)
    message_dims = (PEERS * 8, GROUPS * WIDE + 128)
    message = pl.pallas_call(
        embed_kernel,
        in_specs=[outside] * 7,
        out_specs=outside,
        out_shape=shape(message_dims, BF16),
        scratch_shapes=[
            pltpu.VMEM(tokens.shape, BF16),
            pltpu.VMEM((2, embed_weight.shape[0], WIDE), BF16),
            pltpu.VMEM((2, TOK), BF16),
            pltpu.VMEM((2, 12), BF16),
            pltpu.VMEM((1, 2), BF16),
            pltpu.VMEM((2, 128), jnp.int32),
            pltpu.VMEM((PAIRS, 13), F32),
            pltpu.VMEM((2 * TOK, WIDE), BF16),
            pltpu.VMEM(message_dims, BF16),
            pltpu.SemaphoreType.DMA((12,)),
        ],
        compiler_params=params_for(24),
        name="embed",
    )(hbm(tokens), hbm(embed_weight), hbm(depth_map[0]), hbm(cameras[0]), hbm(focal_len),
      hbm(jnp.swapaxes(pair_graph[0], 0, 1)), hbm(pair_params[0]))
    across = exchange(message, ("x", "c"))
    tile = lax.dynamic_slice(across, (lax.axis_index("z") * PEERS, GROUPS * WIDE), (8, 128))
    spread = exchange(across, ("z", "y"))
    long_rows, short_rows, own, graph = pl.pallas_call(
        index_kernel,
        in_specs=[scalar, inside],
        out_specs=(inside,) * 4,
        out_shape=(
            shape((PEERS * REFS * 8, 1), jnp.int32),
            shape((PEERS * REFS * 4, 1), jnp.int32),
            shape((16, 1), jnp.int32),
            shape((1, PEERS * REFS), jnp.int32),
        ),
        compiler_params=params_for(20),
        cost_estimate=pl.CostEstimate(flops=500000000, bytes_accessed=2000000, transcendentals=0),
        name="index",
    )(rank.reshape(1), tile)

    head_rows = jnp.pad(jnp.swapaxes(point_heads, 1, 2), ((0, 0), (0, 12), (0, 0)))
    square = shape((2, DD, DD), BF16)
    fold, query, key = pl.pallas_call(
        fold_kernel,
        in_specs=[inside, outside, outside, outside],
        out_specs=(inside, inside, inside),
        out_shape=(shape((2, HEADS * 16, DD), BF16), square, square),
        scratch_shapes=[
            pltpu.VMEM((2, DD, DD), BF16),
            pltpu.VMEM((2, DD, DD), BF16),
            pltpu.SemaphoreType.DMA((8,)),
        ],
        compiler_params=params_for(20),
        cost_estimate=pl.CostEstimate(flops=2000000000, bytes_accessed=6000000, transcendentals=0),
        name="fold",
    )(head_rows, hbm(cross_out), hbm(cross_keyval), hbm(cross_query))

    count = PEERS * REFS * PIECE
    outgoing, my_geo, view_par = pl.pallas_call(
        select_kernel,
        in_specs=[scalar] + [inside] * 4 + [pl.BlockSpec(memory_space=pl.ANY)],
        out_specs=(outside, inside, inside),
        out_shape=(
            shape((count, WIDE), BF16),
            shape((REFS, 256), F32),
            shape((REFS, 128), F32),
        ),
        scratch_shapes=[pltpu.VMEM((count, WIDE), BF16), pltpu.SemaphoreType.DMA((PEERS // 32,))],
        compiler_params=params_for(28),
        name="select",
    )(rank.reshape(1), spread, long_rows, short_rows, own, fold)
    rows = exchange(outgoing, PLANE)

    tokens_of = pltpu.VMEM((2, PAIRS * TOK, DD), BF16)
    points, grads = pl.pallas_call(
        decode_kernel,
        in_specs=[inside] * 7,
        out_specs=(inside, inside),
        out_shape=(shape((REFS, 4, TOK), F32), shape((PEERS * REFS, 256), BF16)),
        scratch_shapes=[
            pltpu.VMEM((4, REFS, TOK), F32),
            tokens_of,
            tokens_of,
            tokens_of,
            tokens_of,
            pltpu.VMEM((2, PAIRS, HEADS * 16, TOK), BF16),
            pltpu.VMEM((2, PAIRS, 8, TOK), F32),
        ],
        compiler_params=params_for(28),
        name="decode",
    )(rows, query, key, fold, head_rows, my_geo, view_par)

    own_grad, square = pl.pallas_call(
        combine_kernel,
        in_specs=[scalar, inside, inside],
        out_shape=(shape((16, 256), F32), shape((groups, 128), F32)),
        compiler_params=params_for(16),
        name="combine",
    )(rank.reshape(1), graph, exchange(grads, PLANE))
    own_grad = lax.ppermute(own_grad, PLANE + ("z",), HOME)
    points = lax.ppermute(points, PLANE + ("z",), HOME)
    total = groups * PEERS * (2 * (TOK + 12) + 13 * PAIRS)
    new_depth, new_cameras, new_params, points = pl.pallas_call(
        functools.partial(update_kernel, float(total)),
        out_shape=(shape((2, TOK), F32), shape((2, 12), F32), shape((PAIRS, 13), F32), shape(points.shape, F32)),
        compiler_params=params_for(16),
        name="update",
    )(exchange(square, "z"), own_grad, depth_map[0], cameras[0], pair_params[0], points)
    return (
        points.reshape(1, PAIRS, 2, 4, TOK),
        new_depth[None],
        new_cameras[None],
        new_params[None],
    )


def solution(mesh):
    axes = ("x", "c", "y", "z")
    split = Mesh(np.asarray(mesh.devices).reshape(4, 2, 4, 8), axes)
    grp, dev = ("x", "c"), ("y", "z")
    placed = (
        P(grp, dev, None, None),
        P(grp, dev),
        P(grp, dev, None),
        P(grp, dev, None),
        P(grp, None, None),
        P(grp, dev, None),
        P(),
        P(),
        P(),
        P(),
        P(),
    )
    return jax.shard_map(
        on_device,
        mesh=split,
        in_specs=placed,
        out_specs=(
            P(grp, dev, None, None, None),
            P(grp, dev, None),
            P(grp, dev, None),
            P(grp, dev, None),
        ),
        check_vma=False,
    )
```
